128 devices in a mesh: rows: 4 (over x), prefix: 32 (over z, y, core).
Axes of the slice: x: 4, y: 4, z: 4, core: 2. Of those that a mesh axis runs over, the one named last changes fastest.
Arguments:
- queries: bfloat16 [4, 128, 32, 128], P(None, ('rows', 'prefix')), may hold values from -16 to 16
- new_kv: bfloat16 [2, 4, 128, 16, 128], P(None, None, ('rows', 'prefix')), may hold values from -16 to 16
- suffix_kv: bfloat16 [2, 128, 256, 16, 128], P(None, ('rows', 'prefix')), may hold values from -16 to 16
- suffix_len: int32 [128], P(('rows', 'prefix')), may hold values from 1 to 256, as said below
- prefix_len: int32 [8], replicated, may hold values from 19457 to 40960, as said below
- prefix_kv: bfloat16 [2, 320, 16, 1024, 128], P(None, 'prefix', 'rows'), may hold values from -16 to 16
- block_prompt: int32 [32, 10], P('prefix'), may hold values from 0 to 7, as said below
- block_index: int32 [32, 10], P('prefix'), may hold values from 0 to 39, as said below
- block_count: int32 [32], P('prefix'), may hold values from 1 to 10, as said below
Outputs:
- attention: bfloat16 [4, 128, 4096], P(None, ('rows', 'prefix'))
The draws below stay inside these ranges and needn't reach their ends.
Inputs may be any that keep to these rules, and one draw needn't show every extreme that they name: `block_count`: some owner uses all 10 slots in every draw. `block_prompt`: 0 in unused slots; every block of every prompt lies in exactly one used slot; an owner's used slots hold only blocks of the prompt of its first used slot and of the prompt of its last used slot. `block_index`: 0 in unused slots; a prompt's blocks are numbered from 0; some prompt has 16 * 10 // 4 blocks in every draw. Prompt p has exactly ceil(prefix_len[p] / 1024) blocks; the longest prompt reaches the maximum in every draw. `suffix_len`: some row has 256 in every draw.
All inputs are finite; a program needn't handle non-finite values.
Results may differ from the reference program's by a relative error of at most 0.004.
Values may be sent and summed in bfloat16 or wider, within the bound.
A program may use at most 128 MiB of HBM per device.

```python
import jax
import jax.numpy as jnp
from jax import lax

H = 32
KV = 16
HD = 128
STEPS = 4
SAMPLES = 16
BLOCK = 1024
BLK_CAP = 10
SUF = 256
ROWS = 128
PROMPTS = 8
N_ROWS = 4
N_PREFIX = 32


def shared_parts(key):
    direction = jnp.clip(jax.random.normal(jax.random.fold_in(key, 101), (ROWS, HD), jnp.float32), -3.0, 3.0)
    jitter = jnp.clip(jax.random.normal(jax.random.fold_in(key, 102), (STEPS, ROWS, H, HD), jnp.float32), -3.0, 3.0)
    return (direction, jitter)


def block_layout(key):
    key = jax.random.fold_in(key, 200)
    most = SAMPLES * BLK_CAP // N_ROWS
    least = max(most // 2, 1)
    prompt_ids = jnp.arange(PROMPTS, dtype=jnp.int32)
    blocks = jax.random.randint(jax.random.fold_in(key, 1), (PROMPTS,), least, most + 1, dtype=jnp.int32)
    longest = jax.random.randint(jax.random.fold_in(key, 2), (), 0, PROMPTS, dtype=jnp.int32)
    blocks = jnp.where(prompt_ids == longest, most, blocks).astype(jnp.int32)
    overall = jnp.sum(blocks)
    starts = (jnp.cumsum(blocks) - blocks).astype(jnp.int32)
    order = jax.random.permutation(jax.random.fold_in(key, 3), N_PREFIX).astype(jnp.int32)
    rank = jnp.argsort(order).astype(jnp.int32)
    ranks = jnp.arange(N_PREFIX, dtype=jnp.int32)
    by_rank = 1 + jnp.clip(overall - N_PREFIX - ranks * (BLK_CAP - 1), 0, BLK_CAP - 1)
    rank_offsets = jnp.cumsum(by_rank) - by_rank
    counts = by_rank[rank].astype(jnp.int32)
    offsets = rank_offsets[rank].astype(jnp.int32)
    column = jnp.arange(BLK_CAP, dtype=jnp.int32)
    global_block = offsets[:, None] + column[None, :]
    in_use = column[None, :] < counts[:, None]
    prompt = jnp.sum((global_block[:, :, None] >= starts[None, None, 1:]).astype(jnp.int32), axis=-1)
    prompt = jnp.clip(prompt, 0, PROMPTS - 1)
    block_number = global_block - starts[prompt]
    prompt = jnp.where(in_use, prompt, 0).astype(jnp.int32)
    block_number = jnp.where(in_use, block_number, 0).astype(jnp.int32)
    trim = jax.random.randint(jax.random.fold_in(key, 4), (PROMPTS,), 0, BLOCK, dtype=jnp.int32)
    trim = jnp.where(prompt_ids == longest, 0, trim)
    lengths = blocks * BLOCK - trim
    return (counts, prompt, block_number, lengths.astype(jnp.int32))


def draw_queries(key, part):
    direction, jitter = shared_parts(key)
    result = direction[None, :, None, :] + jitter
    return result.astype(jnp.bfloat16)


def draw_new_kv(key, part):
    direction, jitter = shared_parts(key)
    key = jax.random.fold_in(key, 2)
    aligned = 0.45 * (direction[None, :, None, :] + jitter[:, :, ::H // KV, :])
    own_keys = aligned + 0.5 * jnp.clip(jax.random.normal(jax.random.fold_in(key, 1), (STEPS, ROWS, KV, HD), jnp.float32), -4.0, 4.0)
    own_values = jnp.clip(jax.random.normal(jax.random.fold_in(key, 2), (STEPS, ROWS, KV, HD), jnp.float32), -4.0, 4.0)
    return jnp.stack([own_keys, own_values]).astype(jnp.bfloat16)


def draw_suffix_kv(key, part):
    direction, jitter = shared_parts(key)
    key = jax.random.fold_in(key, 3)
    cache_keys = 0.5 * direction[:, None, None, :] + 0.8 * jnp.clip(jax.random.normal(jax.random.fold_in(key, 1), (ROWS, SUF, KV, HD), jnp.float32), -4.0, 4.0)
    cache_values = jnp.clip(jax.random.normal(jax.random.fold_in(key, 2), (ROWS, SUF, KV, HD), jnp.float32), -4.0, 4.0)
    return jnp.stack([cache_keys.astype(jnp.bfloat16), cache_values.astype(jnp.bfloat16)])


def draw_prefix_kv(key, part):
    key = jax.random.fold_in(key, 4)
    slot_total = N_PREFIX * BLK_CAP
    cache_keys = jnp.clip(jax.random.normal(jax.random.fold_in(key, 1), (slot_total, KV, BLOCK, HD), jnp.float32), -4.0, 4.0)
    cache_keys = cache_keys.astype(jnp.bfloat16)
    cache_values = jnp.clip(jax.random.normal(jax.random.fold_in(key, 2), (slot_total, KV, BLOCK, HD), jnp.float32), -4.0, 4.0).astype(jnp.bfloat16)
    return jnp.stack([cache_keys, cache_values])


def draw_suffix_len(key, part):
    key = jax.random.fold_in(key, 5)
    lengths = jax.random.randint(jax.random.fold_in(key, 1), (ROWS,), 1, SUF + 1, dtype=jnp.int32)
    fullest = jax.random.randint(jax.random.fold_in(key, 2), (), 0, ROWS, dtype=jnp.int32)
    return jnp.where(jnp.arange(ROWS, dtype=jnp.int32) == fullest, SUF, lengths).astype(jnp.int32)


def draw_prefix_len(key, part):
    return block_layout(key)[3]


def draw_block_prompt(key, part):
    return block_layout(key)[1]


def draw_block_index(key, part):
    return block_layout(key)[2]


def draw_block_count(key, part):
    return block_layout(key)[0]


def setup_inputs(seed: int = 0) -> dict:
    keys = jax.random.split(jax.random.key(seed), 10)
    return {
        "queries": draw_queries(jax.random.fold_in(keys[9], 71), 0),
        "new_kv": draw_new_kv(jax.random.fold_in(keys[9], 71), 0),
        "suffix_kv": draw_suffix_kv(jax.random.fold_in(keys[9], 71), 0),
        "suffix_len": draw_suffix_len(jax.random.fold_in(keys[9], 71), 0),
        "prefix_len": draw_prefix_len(jax.random.fold_in(keys[9], 71), 0),
        "prefix_kv": draw_prefix_kv(jax.random.fold_in(keys[9], 71), 0),
        "block_prompt": draw_block_prompt(jax.random.fold_in(keys[9], 71), 0),
        "block_index": draw_block_index(jax.random.fold_in(keys[9], 71), 0),
        "block_count": draw_block_count(jax.random.fold_in(keys[9], 71), 0),
    }


masked_score = -1.0e30
score_scale = 168.0 ** -0.5


def rounded(weights):
    narrow = lax.optimization_barrier(weights.astype(jnp.bfloat16))
    return narrow.astype(jnp.float32)


def reference(queries, new_kv, suffix_kv, suffix_len, prefix_len, prefix_kv, block_prompt, block_index, block_count):
    group = H // KV
    query_all = queries.astype(jnp.float32).reshape(STEPS, PROMPTS, SAMPLES, KV, group, HD)
    slot_total = N_PREFIX * BLK_CAP
    flat_prompt = block_prompt.reshape(slot_total).astype(jnp.int32)
    flat_block = block_index.reshape(slot_total).astype(jnp.int32)
    slot_live = (jnp.arange(slot_total, dtype=jnp.int32) % BLK_CAP) < jnp.repeat(block_count.astype(jnp.int32), BLK_CAP)
    positions = jnp.arange(BLOCK, dtype=jnp.int32)
    peak_init = jnp.full((PROMPTS, STEPS, SAMPLES, KV, group), masked_score, jnp.float32)
    mass_init = jnp.zeros((PROMPTS, STEPS, SAMPLES, KV, group), jnp.float32)
    sum_init = jnp.zeros((PROMPTS, STEPS, SAMPLES, KV, group, HD), jnp.float32)

    def visit(slot_number, carry):
        peak_all, mass_all, sum_all = carry
        prompt = flat_prompt[slot_number]
        live = slot_live[slot_number] & (flat_block[slot_number] * BLOCK + positions < prefix_len[prompt])
        chosen = lax.dynamic_index_in_dim(query_all, prompt, 1, keepdims=False)
        key_block = prefix_kv[0, slot_number].astype(jnp.float32)
        value_block = prefix_kv[1, slot_number].astype(jnp.float32)
        scores = jnp.einsum("tskgd,kbd->tskgb", chosen, key_block) * score_scale
        scores = jnp.where(live, scores, masked_score)
        block_peak = jnp.max(scores, axis=-1)
        weights = rounded(jnp.where(live, jnp.exp(scores - block_peak[..., None]), 0.0))
        block_mass = jnp.sum(weights, axis=-1)
        block_sum = jnp.einsum("tskgb,kbd->tskgd", weights, value_block)
        old_peak = lax.dynamic_index_in_dim(peak_all, prompt, 0, keepdims=False)
        old_mass = lax.dynamic_index_in_dim(mass_all, prompt, 0, keepdims=False)
        old_sum = lax.dynamic_index_in_dim(sum_all, prompt, 0, keepdims=False)
        new_peak = jnp.maximum(old_peak, block_peak)
        keep_old = jnp.exp(old_peak - new_peak)
        take_new = jnp.exp(block_peak - new_peak)
        peak_all = lax.dynamic_update_index_in_dim(peak_all, new_peak, prompt, 0)
        mass_all = lax.dynamic_update_index_in_dim(mass_all, keep_old * old_mass + take_new * block_mass, prompt, 0)
        sum_all = lax.dynamic_update_index_in_dim(sum_all, keep_old[..., None] * old_sum + take_new[..., None] * block_sum, prompt, 0)
        return peak_all, mass_all, sum_all

    peak_all, mass_all, sum_all = lax.fori_loop(0, slot_total, visit, (peak_init, mass_init, sum_init))
    prefix_peak = peak_all.transpose(1, 0, 2, 3, 4).reshape(STEPS, ROWS, KV, group)
    prefix_mass = mass_all.transpose(1, 0, 2, 3, 4).reshape(STEPS, ROWS, KV, group)
    prefix_sum = sum_all.transpose(1, 0, 2, 3, 4, 5).reshape(STEPS, ROWS, KV, group, HD)

    query_rows = queries.astype(jnp.float32).reshape(STEPS, ROWS, KV, group, HD)
    far = jnp.einsum("trkgd,rpkd->trkgp", query_rows, suffix_kv[0].astype(jnp.float32)) * score_scale
    near = jnp.einsum("trkgd,prkd->trkgp", query_rows, new_kv[0].astype(jnp.float32)) * score_scale
    far_live = (jnp.arange(SUF, dtype=jnp.int32)[None, :] < suffix_len[:, None])[None, :, None, None, :]
    step_ids = jnp.arange(STEPS, dtype=jnp.int32)
    near_live = (step_ids[None, :] <= step_ids[:, None])[:, None, None, None, :]
    far = jnp.where(far_live, far, masked_score)
    near = jnp.where(near_live, near, masked_score)
    own_peak = jnp.maximum(jnp.max(far, axis=-1), jnp.max(near, axis=-1))
    far_weights = rounded(jnp.where(far_live, jnp.exp(far - own_peak[..., None]), 0.0))
    near_weights = rounded(jnp.where(near_live, jnp.exp(near - own_peak[..., None]), 0.0))
    own_mass = jnp.sum(far_weights, axis=-1) + jnp.sum(near_weights, axis=-1)
    own_sum = jnp.einsum("trkgp,rpkd->trkgd", far_weights, suffix_kv[1].astype(jnp.float32))
    own_sum = own_sum + jnp.einsum("trkgp,prkd->trkgd", near_weights, new_kv[1].astype(jnp.float32))

    top = jnp.maximum(prefix_peak, own_peak)
    from_prefix = jnp.exp(prefix_peak - top)
    from_own = jnp.exp(own_peak - top)
    numer = from_prefix[..., None] * prefix_sum + from_own[..., None] * own_sum
    denom = from_prefix * prefix_mass + from_own * own_mass
    return (numer / denom[..., None]).reshape(STEPS, ROWS, H * HD).astype(jnp.bfloat16)
```

```python
import functools
import math

import jax
import jax.numpy as jnp
from jax import lax
from jax.experimental import pallas as pl
from jax.experimental.pallas import tpu as pltpu
from jax.sharding import PartitionSpec as P

MESH = pl.DeviceIdType.MESH
SAMPLES = 16
masked_score = -1e30
exponent = 168.0 ** (-0.5) * math.log2(math.e)
f32 = jnp.float32
bf16 = jnp.bfloat16
NT = (((1,), (1,)), ((), ()))
NN = (((1,), (0,)), ((), ()))
UNROLL = 5


def iota(shape, dim):
    return lax.broadcasted_iota(jnp.int32, shape, dim)


def kernel(
    n_x,
    n_i,
    block_len,
    slots,
    prompt_ref,
    index_ref,
    count_ref,
    prefix_len_ref,
    suffix_len_ref,
    q_ref,
    new_ref,
    suffix_hbm,
    prefix_hbm,
    out_ref,
    kv,
    suf,
    q_own,
    q_x,
    q_src,
    q_all,
    q_prompt,
    own_s,
    own_acc,
    own_m,
    own_l,
    accs,
    ms,
    ls,
    acc_sel,
    m_sel,
    l_sel,
    part,
    part_in,
    stat,
    stat_in,
    fin,
    fin_in,
    kv_sem,
    suf_sem,
    x_send,
    x_recv,
    q_send,
    q_recv,
    part_send,
    part_recv,
    stat_send,
    stat_recv,
    fin_send,
    fin_recv,
):
    me_x = lax.axis_index("rows")
    me_i = lax.axis_index("prefix")
    kv_local = kv.shape[0]
    rows = q_ref.shape[0]

    suf_copy = pltpu.make_async_copy(suffix_hbm, suf, suf_sem)
    suf_copy.start()
    kv_copies = [
        pltpu.make_async_copy(prefix_hbm.at[:, :, k], kv.at[k], kv_sem.at[k])
        for k in range(kv_local)
    ]
    for copy in kv_copies:
        copy.start()

    def peer(d):
        return lax.rem(me_i + d, n_i)

    def mate(d):
        return lax.rem(me_x + d, n_x)

    barrier = pltpu.get_barrier_semaphore()

    def greet(d, carry):
        pl.semaphore_signal(barrier, inc=1, device_id=(me_x, peer(d)), device_id_type=MESH)
        return carry

    lax.fori_loop(1, n_i, greet, 0)
    for d in range(1, n_x):
        pl.semaphore_signal(barrier, inc=1, device_id=(mate(d), me_i), device_id_type=MESH)

    r = iota((rows, rows), 0)
    c = iota((rows, rows), 1)
    source = (lax.rem(r, 8) // 2) * 32 + (r // 8) * 2 + lax.rem(r, 2)
    order = jnp.where(c == source, 1.0, 0.0).astype(bf16)
    q_mine = lax.dot_general(order, q_ref[...], NN, preferred_element_type=f32).astype(bf16)
    q_own[...] = q_mine.reshape(n_x, 32, 128)
    stat[...] = jnp.zeros_like(stat)
    acc_sel[0] = jnp.zeros((rows, 128), f32)
    m_sel[0] = jnp.full((rows, 128), masked_score, f32)
    l_sel[0] = jnp.zeros((rows, 128), f32)

    pl.semaphore_wait(barrier, n_i - 1 + n_x - 1)

    def waiter(ref, send, recv):
        return pltpu.make_async_remote_copy(
            src_ref=ref,
            dst_ref=ref,
            send_sem=send,
            recv_sem=recv,
            device_id=(me_x, peer(1)),
            device_id_type=MESH,
        )

    for d in range(1, n_x):
        g = mate(d)
        pltpu.make_async_remote_copy(
            src_ref=q_own.at[g],
            dst_ref=q_x.at[me_x],
            send_sem=x_send,
            recv_sem=x_recv,
            device_id=(g, me_i),
            device_id_type=MESH,
        ).start()
    q_x[me_x] = q_own[me_x]
    waiter(q_x.at[pl.ds(0, n_x - 1)], x_send, x_recv).wait_recv()
    gathered = q_x[...].astype(f32).reshape(n_x, kv_local, 8, 128).transpose(1, 0, 2, 3)
    gathered = gathered.reshape(kv_local, n_x * 8, 128).astype(bf16)
    q_src[...] = gathered
    for k in range(kv_local):
        q_all[k, me_i] = gathered[k]
    for k in range(kv_local):

        def push_q(d, carry, k=k):
            pltpu.make_async_remote_copy(
                src_ref=q_src.at[k],
                dst_ref=q_all.at[k, me_i],
                send_sem=q_send.at[k],
                recv_sem=q_recv.at[k],
                device_id=(me_x, peer(d)),
                device_id_type=MESH,
            ).start()
            return carry

        lax.fori_loop(1, n_i, push_q, 0)

    suf_copy.wait()
    chunk = own_s.shape[2]
    chunks = own_s.shape[0]
    suffix_len = suffix_len_ref[0]
    row_head = iota((rows, 1), 0) // 8
    row_step = lax.rem(iota((rows, 1), 0), 8) // 2
    near = lax.dot_general(q_mine, new_ref[0], NT, preferred_element_type=f32)
    lane = iota((1, near.shape[1]), 1)
    near_live = (lax.rem(lane, 16) == row_head) & (lane // 16 <= row_step)
    near = jnp.where(near_live, near, masked_score)
    lane = iota((1, chunk), 1)
    same_head = lax.rem(lane, 16) == row_head

    def far_scores(n, peak):
        s = lax.dot_general(
            q_mine, suf[0, pl.ds(n * chunk, chunk)], NT, preferred_element_type=f32
        )
        live = same_head & (n * (chunk // 16) + lane // 16 < suffix_len)
        s = jnp.where(live, s, masked_score)
        own_s[n] = s
        return jnp.maximum(peak, jnp.max(s, axis=1, keepdims=True))

    own_peak = lax.fori_loop(0, chunks, far_scores, jnp.max(near, axis=1, keepdims=True))
    near_w = jnp.exp2((near - own_peak) * exponent).astype(bf16)
    near_sum = lax.dot_general(near_w, new_ref[1], NN, preferred_element_type=f32)
    near_mass = jnp.sum(near_w.astype(f32), axis=1, keepdims=True)
    ones = jnp.ones((chunk, 128), bf16)

    def far_sums(n, carry):
        total, mass = carry
        w = jnp.exp2((own_s[n] - own_peak) * exponent).astype(bf16)
        values = jnp.concatenate([suf[1, pl.ds(n * chunk, chunk)], ones], axis=1)
        both = lax.dot_general(w, values, NN, preferred_element_type=f32)
        return total + both[:, :128], mass + both[:, 128:]

    total, mass = lax.fori_loop(
        0, chunks, far_sums, (near_sum, jnp.broadcast_to(near_mass, (rows, 128)))
    )
    own_acc[...] = total
    own_l[...] = mass
    own_m[...] = jnp.broadcast_to(own_peak, (rows, 128))

    count = count_ref[0]
    prompt_a = prompt_ref[0, 0]
    prompt_b = prompt_ref[0, jnp.maximum(count - 1, 0)]
    column = iota((1, block_len), 1)
    ones = jnp.ones((block_len, 128), bf16)
    lane = iota((1, 1, 128), 2)

    def pick(p):
        return jnp.where(prompt_a == p, 1, jnp.where(prompt_b == p, 2, 0))

    for k in range(kv_local):
        waiter(q_all.at[k, pl.ds(0, n_i - 1)], q_send.at[k], q_recv.at[k]).wait_recv()
        for half in range(2):
            v = q_all[k, pl.ds(half * SAMPLES, SAMPLES)].astype(f32)
            v = v.reshape(SAMPLES, n_x, 8, 128)
            for x in range(n_x):
                q_prompt[2 * x + half] = v[:, x].reshape(rows, 128).astype(bf16)
        kv_copies[k].wait()

        def visit(step, carry, k=k):
            for u in range(UNROLL):
                j = step * UNROLL + u
                prompt = prompt_ref[0, j]
                live = prefix_len_ref[prompt] - index_ref[0, j] * block_len
                live = jnp.where(j < count, live, 0)
                s = lax.dot_general(
                    q_prompt[prompt], kv[k, 0, j], NT, preferred_element_type=f32
                )
                s = jnp.where(column < live, s, masked_score)
                m = jnp.max(s, axis=1, keepdims=True)
                w = jnp.exp2((s - m) * exponent).astype(bf16)
                values = jnp.concatenate([kv[k, 1, j], ones], axis=1)
                both = lax.dot_general(w, values, NN, preferred_element_type=f32)
                accs[j] = both[:, :128]
                ls[j] = both[:, 128:]
                ms[j] = jnp.broadcast_to(m, (rows, 128))
            return carry

        lax.fori_loop(0, slots // UNROLL, visit, 0)

        for place, prompt in ((1, prompt_a), (2, prompt_b)):
            outside = [jnp.where(prompt_ref[0, j] == prompt, 0.0, masked_score) for j in range(slots)]
            peak = ms[0] + outside[0]
            for j in range(1, slots):
                peak = jnp.maximum(peak, ms[j] + outside[j])
            total = jnp.zeros((rows, 128), f32)
            mass = jnp.zeros((rows, 128), f32)
            for j in range(slots):
                take = jnp.exp2((ms[j] + outside[j] - peak) * exponent)
                total = total + take * accs[j]
                mass = mass + take * ls[j]
            acc_sel[place] = total
            m_sel[place] = peak
            l_sel[place] = mass

        for half in range(2):
            span = pl.ds(half * SAMPLES, SAMPLES)
            st = stat[span]
            parts = []
            for x in range(n_x):
                which = pick(2 * x + half)
                parts.append(acc_sel[which].reshape(SAMPLES, 1, 8, 128))
                at = x * 32 + k * 8
                st = jnp.where(lane == at, m_sel[which].reshape(SAMPLES, 8, 128), st)
                st = jnp.where(lane == at + 1, l_sel[which].reshape(SAMPLES, 8, 128), st)
            stat[span] = st
            block = jnp.concatenate(parts, axis=1).reshape(SAMPLES, n_x * 8, 128)
            part[k, span] = block.astype(bf16)

        def push_part(d, carry, k=k):
            to = peer(d)
            pltpu.make_async_remote_copy(
                src_ref=part.at[k, to],
                dst_ref=part_in.at[k, me_i],
                send_sem=part_send.at[k],
                recv_sem=part_recv.at[k],
                device_id=(me_x, to),
                device_id_type=MESH,
            ).start()
            return carry

        def push_stat(d, carry):
            to = peer(d)
            pltpu.make_async_remote_copy(
                src_ref=stat.at[to],
                dst_ref=stat_in.at[me_i],
                send_sem=stat_send,
                recv_sem=stat_recv,
                device_id=(me_x, to),
                device_id_type=MESH,
            ).start()
            return carry

        if k == kv_local - 1:
            lax.fori_loop(1, n_i, push_stat, 0)
        lax.fori_loop(1, n_i, push_part, 0)
        part_in[k, me_i] = part[k, me_i]
    stat_in[me_i] = stat[me_i]

    stat_wait = waiter(stat_in.at[pl.ds(0, n_i - 1)], stat_send, stat_recv)
    stat_wait.wait_recv()
    st = stat_in[...]
    peak = jnp.max(st, axis=0)
    factor = jnp.exp2((st - peak) * exponent)
    mass_at = pltpu.roll(st.reshape(n_i * 8, 128), 127, 1).reshape(n_i, 8, 128)
    mass = jnp.sum(factor * mass_at, axis=0)
    stat_in[...] = factor
    part_waits = []
    for k in range(kv_local):
        part_wait = waiter(part_in.at[k, pl.ds(0, n_i - 1)], part_send.at[k], part_recv.at[k])
        part_wait.wait_recv()
        part_waits.append(part_wait)

    def add_owner(o, carry):
        carry = list(carry)
        f = stat_in[o]
        for k in range(kv_local):
            v = part_in[k, o].astype(f32)
            for x in range(n_x):
                at = x * 32 + k * 8
                n = k * n_x + x
                carry[n] = carry[n] + f[:, at : at + 1] * v[x * 8 : x * 8 + 8]
        return tuple(carry)

    sums = lax.fori_loop(
        0, n_i, add_owner, tuple(jnp.zeros((8, 128), f32) for _ in range(kv_local * n_x)), unroll=4
    )
    lane = iota((1, 128), 1)
    both = jnp.where(lax.rem(lane, 8) == 1, pltpu.roll(mass, 1, 1), peak)
    for x in range(n_x):
        for k in range(kv_local):
            fin[x, k * 8 : k * 8 + 8] = sums[k * n_x + x]
        fin[x, kv_local * 8 : kv_local * 8 + 8] = pltpu.roll(both, (128 - 32 * x) % 128, 1) if x else both
    for d in range(1, n_x):
        x = mate(d)
        pltpu.make_async_remote_copy(
            src_ref=fin.at[x],
            dst_ref=fin_in.at[me_x],
            send_sem=fin_send,
            recv_sem=fin_recv,
            device_id=(x, me_i),
            device_id_type=MESH,
        ).start()
    fin_in[me_x] = fin[me_x]
    fin_wait = waiter(fin_in.at[pl.ds(0, n_x - 1)], fin_send, fin_recv)
    fin_wait.wait_recv()

    result = []
    for g in range(n_x):
        st = fin_in[g, kv_local * 8 : kv_local * 8 + 8]
        for k in range(kv_local):
            at = (g * kv_local + k) * 8
            span = slice(at, at + 8)
            prefix_peak = st[:, k * 8 : k * 8 + 1]
            prefix_mass = st[:, k * 8 + 1 : k * 8 + 2]
            mine = own_m[span, :]
            top = jnp.maximum(prefix_peak, mine)
            from_prefix = jnp.exp2((prefix_peak - top) * exponent)
            from_own = jnp.exp2((mine - top) * exponent)
            numer = from_prefix * fin_in[g, k * 8 : k * 8 + 8] + from_own * own_acc[span, :]
            denom = from_prefix * prefix_mass + from_own * own_l[span, :]
            result.append(numer / denom)
    result = jnp.concatenate(result, axis=0).astype(bf16)
    source = lax.rem(r, 32) // 2 * 8 + (r // 32) * 2 + lax.rem(r, 2)
    order = jnp.where(c == source, 1.0, 0.0).astype(bf16)
    out_ref[...] = lax.dot_general(order, result, NN, preferred_element_type=f32).astype(bf16)

    waiter(q_x.at[pl.ds(0, n_x - 1)], x_send, x_recv).wait_send()
    for k in range(kv_local):
        waiter(q_all.at[k, pl.ds(0, n_i - 1)], q_send.at[k], q_recv.at[k]).wait_send()
        part_waits[k].wait_send()
    stat_wait.wait_send()
    fin_wait.wait_send()


def local(
    n_x,
    n_i,
    queries,
    new_kv,
    suffix_kv,
    suffix_len,
    prefix_len,
    prefix_kv,
    block_prompt,
    block_index,
    block_count,
):
    steps, rows_dev, heads, width = queries.shape
    slots, kv_local, block_len = prefix_kv.shape[1:4]
    rows = steps * heads
    q = queries.reshape(rows, width)
    new = new_kv.reshape(2, -1, width)
    suffix = suffix_kv.reshape(2, -1, width)
    keys = suffix.shape[1]
    chunk = 1024
    smem = pl.BlockSpec(memory_space=pltpu.SMEM)
    vmem = pl.BlockSpec(memory_space=pltpu.VMEM)
    hbm = pl.BlockSpec(memory_space=pl.ANY)
    dma = pltpu.SemaphoreType.DMA
    out = pl.pallas_call(
        functools.partial(kernel, n_x, n_i, block_len, slots),
        out_shape=jax.ShapeDtypeStruct((rows, width), bf16),
        in_specs=[smem] * 5 + [vmem, vmem, hbm, hbm],
        out_specs=vmem,
        scratch_shapes=[
            pltpu.VMEM((kv_local, 2, slots, block_len, width), bf16),
            pltpu.VMEM((2, keys, width), bf16),
            pltpu.VMEM((n_x, 32, width), bf16),
            pltpu.VMEM((n_x, 32, width), bf16),
            pltpu.VMEM((kv_local, n_x * 8, width), bf16),
            pltpu.VMEM((kv_local, n_i, n_x * 8, width), bf16),
            pltpu.VMEM((8, rows, width), bf16),
            pltpu.VMEM((keys // chunk, rows, chunk), f32),
            pltpu.VMEM((rows, width), f32),
            pltpu.VMEM((rows, width), f32),
            pltpu.VMEM((rows, width), f32),
            pltpu.VMEM((slots, rows, width), f32),
            pltpu.VMEM((slots, rows, width), f32),
            pltpu.VMEM((slots, rows, width), f32),
            pltpu.VMEM((3, rows, width), f32),
            pltpu.VMEM((3, rows, width), f32),
            pltpu.VMEM((3, rows, width), f32),
            pltpu.VMEM((kv_local, n_i, n_x * 8, width), bf16),
            pltpu.VMEM((kv_local, n_i, n_x * 8, width), bf16),
            pltpu.VMEM((n_i, 8, 128), f32),
            pltpu.VMEM((n_i, 8, 128), f32),
            pltpu.VMEM((n_x, (kv_local + 1) * 8, width), f32),
            pltpu.VMEM((n_x, (kv_local + 1) * 8, width), f32),
            dma((kv_local,)),
            dma,
            dma,
            dma,
            dma((kv_local,)),
            dma((kv_local,)),
            dma((kv_local,)),
            dma((kv_local,)),
            dma,
            dma,
            dma,
            dma,
        ],
        compiler_params=pltpu.CompilerParams(
            collective_id=0, has_side_effects=True, vmem_limit_bytes=60 << 20
        ),
        name="decode_attention",
    )(block_prompt, block_index, block_count, prefix_len, suffix_len, q, new, suffix, prefix_kv)
    return out.reshape(steps, rows_dev, heads * width)


def solution(mesh):
    return jax.shard_map(
        functools.partial(local, mesh.shape["rows"], mesh.shape["prefix"]),
        mesh=mesh,
        in_specs=(
            P(None, ("rows", "prefix"), None, None),
            P(None, None, ("rows", "prefix"), None, None),
            P(None, ("rows", "prefix"), None, None, None),
            P(("rows", "prefix")),
            P(),
            P(None, "prefix", "rows", None, None),
            P("prefix", None),
            P("prefix", None),
            P("prefix"),
        ),
        out_specs=P(None, ("rows", "prefix"), None),
        check_vma=False,
    )
```

```python
import functools
import math

import jax
import jax.numpy as jnp
from jax import lax
from jax.experimental import pallas as pl
from jax.experimental.pallas import tpu as pltpu
from jax.sharding import PartitionSpec as P

MESH = pl.DeviceIdType.MESH
SAMPLES = 16
masked_score = -1e30
exponent = 168.0 ** (-0.5) * math.log2(math.e)
f32 = jnp.float32
bf16 = jnp.bfloat16
NT = (((1,), (1,)), ((), ()))
NN = (((1,), (0,)), ((), ()))
X_ORDER = (0, 1, 3, 2)


def iota(shape, dim):
    return lax.broadcasted_iota(jnp.int32, shape, dim)


def kernel(
    n_x,
    n_i,
    block_len,
    slots,
    prompt_hbm,
    index_hbm,
    count_hbm,
    prefix_len_hbm,
    suffix_len_hbm,
    q_hbm,
    new_hbm,
    suffix_hbm,
    prefix_hbm,
    out_ref,
    prompt_ref,
    index_ref,
    count_ref,
    prefix_len_ref,
    suffix_len_ref,
    q_ref,
    new_ref,
    kv,
    suf,
    q_own,
    q_all,
    q_prompt,
    own_s,
    own_acc,
    own_m,
    own_l,
    m_sel,
    packed,
    tag,
    tag_in,
    part,
    part_in,
    stat,
    stat_in,
    fin,
    fin_in,
    int_sem,
    small_sem,
    kv_sem,
    suf_sem,
    q_send,
    q_recv,
    forward_send,
    forward_recv,
    tag_send,
    tag_recv,
    part_send,
    part_recv,
    stat_send,
    stat_recv,
    fin_send,
    fin_recv,
):
    me_x = lax.axis_index("rows")
    me_i = lax.axis_index("prefix")
    me_j = me_i // 2
    me_c = lax.rem(me_i, 2)
    other_c = 1 - me_c
    sibling = (me_x, me_j * 2 + other_c)
    n_j = n_i // 2
    kv_local = kv.shape[0]
    rows = q_ref.shape[0]
    half_j = SAMPLES // 2
    lane = iota((1, 128), 1)
    pairs = kv_local // 2

    def peer(d):
        return lax.rem(me_i + d, n_i)

    def sample(i):
        return lax.rem(i, 2) * half_j + lax.rem(i, SAMPLES) // 2

    def on_core(d):
        return lax.rem(me_j + d, n_j) * 2 + me_c

    def mate(d):
        return lax.rem(me_x + d, n_x)

    barrier = pltpu.get_barrier_semaphore()

    def greet_other(j, carry):
        pl.semaphore_signal(
            barrier, inc=1, device_id=(me_x, j * 2 + other_c), device_id_type=MESH
        )
        return carry

    lax.fori_loop(0, n_j, greet_other, 0)
    for dx in range(n_x):

        def greet(d, carry, dx=dx):
            pl.semaphore_signal(
                barrier, inc=1, device_id=(mate(dx), on_core(d)), device_id_type=MESH
            )
            return carry

        lax.fori_loop(1 if dx == 0 else 0, n_j, greet, 0)

    small_copies = [
        pltpu.make_async_copy(q_hbm, q_ref, small_sem.at[0]),
        pltpu.make_async_copy(new_hbm, new_ref, small_sem.at[1]),
    ]
    int_copies = [
        pltpu.make_async_copy(src, dst, int_sem.at[n])
        for n, (src, dst) in enumerate(
            (
                (prompt_hbm, prompt_ref),
                (index_hbm, index_ref),
                (count_hbm, count_ref),
                (prefix_len_hbm, prefix_len_ref),
                (suffix_len_hbm, suffix_len_ref),
            )
        )
    ]
    suf_copy = pltpu.make_async_copy(suffix_hbm, suf, suf_sem)
    kv_copies = [
        pltpu.make_async_copy(prefix_hbm.at[:, :, k], kv.at[k], kv_sem.at[k])
        for k in range(kv_local)
    ]
    for copy in small_copies + int_copies + [suf_copy]:
        copy.start()

    r = iota((rows, rows), 0)
    c = iota((rows, rows), 1)
    source = lax.rem(r, 4) * 32 + (r // 8) * 2 + lax.rem(r // 4, 2)
    order = jnp.where(c == source, 1.0, 0.0).astype(bf16)
    small_copies[0].wait()
    q_mine = lax.dot_general(order, q_ref[...], NN, preferred_element_type=f32).astype(bf16)
    q_own[...] = q_mine.reshape(n_x, pairs, 16, 128)
    for pair in range(pairs):
        q_all[pair, me_c, me_x, me_j] = q_own[me_x, pair]
    packed[...] = jnp.zeros_like(packed)

    pl.semaphore_wait(barrier, n_x * n_j - 1 + n_j)

    def waiter(ref, send, recv):
        return pltpu.make_async_remote_copy(
            src_ref=ref,
            dst_ref=ref,
            send_sem=send,
            recv_sem=recv,
            device_id=sibling,
            device_id_type=MESH,
        )

    def push(src, dst, send, recv, to):
        pltpu.make_async_remote_copy(
            src_ref=src,
            dst_ref=dst,
            send_sem=send,
            recv_sem=recv,
            device_id=to,
            device_id_type=MESH,
        ).start()

    for pair in range(pairs):
        for dx in X_ORDER:

            def push_q(d, carry, pair=pair, dx=dx):
                x = mate(dx)
                push(
                    q_own.at[x, pair],
                    q_all.at[pair, me_c, me_x, me_j],
                    q_send.at[pair, dx],
                    q_recv.at[pair, dx],
                    (x, on_core(d)),
                )
                return carry

            lax.fori_loop(1 if dx == 0 else 0, n_j, push_q, 0)
    for copy in kv_copies:
        copy.start()

    def q_wait(pair, dx):
        chunks = q_all.at[pair, me_c, 0, pl.ds(0, n_j - 1 if dx == 0 else n_j)]
        return waiter(chunks, q_send.at[pair, dx], q_recv.at[pair, dx])

    for copy in small_copies[1:] + int_copies + [suf_copy]:
        copy.wait()
    count = count_ref[0]
    prompt_a = prompt_ref[0, 0]
    prompt_b = prompt_ref[0, jnp.maximum(count - 1, 0)]
    base = lax.rem(me_i, 8) * 16
    in_first = (lane >= base) & (lane < base + 8)
    in_second = (lane >= base + 8) & (lane < base + 16)
    tag_a = prompt_a.astype(f32)
    tag_b = jnp.where(prompt_b == prompt_a, -1, prompt_b).astype(f32)
    tags = jnp.where(in_first, tag_a, jnp.where(in_second, tag_b, 0.0))
    tag[...] = jnp.broadcast_to(tags, (8, 128))
    tag_in[me_i] = tag[...]

    def push_tag(d, carry):
        push(tag, tag_in.at[me_i], tag_send, tag_recv, (me_x, peer(d)))
        return carry

    lax.fori_loop(1, n_i, push_tag, 0)
    chunk = own_s.shape[2]
    chunks = own_s.shape[0]
    suffix_len = suffix_len_ref[0]
    row_head = iota((rows, 1), 0) // 8
    row_step = lax.rem(iota((rows, 1), 0), 4)
    near = lax.dot_general(q_mine, new_ref[0], NT, preferred_element_type=f32)
    key = iota((1, near.shape[1]), 1)
    near_live = (lax.rem(key, 16) == row_head) & (key // 16 <= row_step)
    near = jnp.where(near_live, near, masked_score)
    key = iota((1, chunk), 1)
    same_head = lax.rem(key, 16) == row_head

    def far_scores(n, peak):
        s = lax.dot_general(
            q_mine, suf[0, pl.ds(n * chunk, chunk)], NT, preferred_element_type=f32
        )
        live = same_head & (n * (chunk // 16) + key // 16 < suffix_len)
        s = jnp.where(live, s, masked_score)
        own_s[n] = s
        return jnp.maximum(peak, jnp.max(s, axis=1, keepdims=True))

    own_peak = lax.fori_loop(0, chunks, far_scores, jnp.max(near, axis=1, keepdims=True))
    near_w = jnp.exp2((near - own_peak) * exponent).astype(bf16)
    near_sum = lax.dot_general(near_w, new_ref[1], NN, preferred_element_type=f32)
    near_mass = jnp.sum(near_w.astype(f32), axis=1, keepdims=True)
    ones = jnp.ones((chunk, 128), bf16)

    def far_sums(n, carry):
        total, mass = carry
        w = jnp.exp2((own_s[n] - own_peak) * exponent).astype(bf16)
        values = jnp.concatenate([suf[1, pl.ds(n * chunk, chunk)], ones], axis=1)
        both = lax.dot_general(w, values, NN, preferred_element_type=f32)
        return total + both[:, :128], mass + both[:, 128:]

    total, mass = lax.fori_loop(
        0, chunks, far_sums, (near_sum, jnp.broadcast_to(near_mass, (rows, 128)))
    )
    own_acc[...] = total
    own_l[...] = mass
    own_m[...] = jnp.broadcast_to(own_peak, (rows, 128))

    column = iota((1, block_len), 1)
    ones = jnp.ones((block_len, 128), bf16)
    in_a = [jnp.where(prompt_ref[0, j] == prompt_a, 1, 0) for j in range(slots)]
    outside_a = outside_b = jnp.full((1, 128), masked_score, f32)
    for j in range(slots):
        inside = jnp.where(prompt_ref[0, j] == prompt_a, 0.0, masked_score)
        outside_a = jnp.where(lane == j, inside, outside_a)
        inside = jnp.where(prompt_ref[0, j] == prompt_b, 0.0, masked_score)
        outside_b = jnp.where(lane == j, inside, outside_b)

    def forward_q(pair):
        for dx in X_ORDER:
            q_wait(pair, dx).wait_recv()
            mine = q_all.at[pair, me_c, lax.rem(me_x + n_x - dx, n_x)]
            push(mine, mine, forward_send.at[pair, dx], forward_recv.at[pair, dx], sibling)

    def push_part(k):
        def one(d, carry):
            to = peer(d)
            push(
                part.at[k, sample(to)],
                part_in.at[k, me_i],
                part_send.at[k],
                part_recv.at[k],
                (me_x, to),
            )
            return carry

        lax.fori_loop(1, n_i, one, 0)
        part_in[k, me_i] = part[k, sample(me_i)]

    def push_stat(d, carry):
        to = peer(d)
        push(stat.at[sample(to)], stat_in.at[me_i], stat_send, stat_recv, (me_x, to))
        return carry

    forward_q(0)
    for k in range(kv_local):
        pair = k // 2
        if k % 2 == 0:
            for dx in X_ORDER:
                waiter(
                    q_all.at[pair, me_c, 0], forward_send.at[pair, dx], forward_recv.at[pair, dx]
                ).wait_recv()
            for half in range(2):
                for x in range(n_x):
                    v = q_all[pair, :, x, pl.ds(half * half_j, half_j)].astype(f32)
                    v = v.reshape(SAMPLES, 2, 8, 128)
                    for n in range(2):
                        q_prompt[n, 2 * x + half] = v[:, n].reshape(rows, 128).astype(bf16)
        elif pair + 1 < pairs:
            forward_q(pair + 1)
        kv_copies[k].wait()

        accs, ms = [], []
        peaks = jnp.full((rows, 128), masked_score, f32)
        masses = jnp.zeros((rows, 128), f32)
        for j in range(slots):
            prompt = prompt_ref[0, j]
            live = prefix_len_ref[prompt] - index_ref[0, j] * block_len
            live = jnp.where(j < count, live, 0)
            s = lax.dot_general(
                q_prompt[k % 2, prompt], kv[k, 0, j], NT, preferred_element_type=f32
            )
            s = jnp.where(column < live, s, masked_score)
            m = jnp.max(s, axis=1, keepdims=True)
            w = jnp.exp2((s - m) * exponent).astype(bf16)
            values = jnp.concatenate([kv[k, 1, j], ones], axis=1)
            both = lax.dot_general(w, values, NN, preferred_element_type=f32)
            accs.append(both[:, :128])
            ms.append(m)
            peaks = jnp.where(lane == j, m, peaks)
            masses = jnp.where(lane == j, both[:, 128:], masses)

        pack = packed[...]
        for place, outside in ((1, outside_a), (2, outside_b)):
            shifted = peaks + outside
            peak = jnp.max(shifted, axis=1, keepdims=True)
            take = jnp.exp2((shifted - peak) * exponent)
            mass = jnp.sum(take * masses, axis=1, keepdims=True)
            m_sel[place] = jnp.broadcast_to(peak, (rows, 128))
            at = (place - 1) * 8 + k * 2
            pack = jnp.where(lane == at, peak, jnp.where(lane == at + 1, mass, pack))
        packed[...] = pack
        total_a = total_b = jnp.zeros((rows, 128), f32)
        for j in range(slots):
            take = jnp.exp2((ms[j] - m_sel[2 - in_a[j]]) * exponent)
            taken = take * accs[j]
            total_a = total_a + jnp.where(in_a[j] == 1, taken, 0.0)
            total_b = total_b + jnp.where(in_a[j] == 1, 0.0, taken)
        parts = [t.reshape(SAMPLES, 8, 128) for t in (total_a, total_b)]
        part[k] = jnp.concatenate(parts, axis=1).astype(bf16)
        push_part(k)

    turned = packed[...].T
    first = pltpu.roll(turned[:8], base, 1)
    second = pltpu.roll(turned[8:16], base + 8, 1)
    for n in range(SAMPLES):
        shift = (128 - 8 * n) % 128
        one, two = (pltpu.roll(a, shift, 1) if shift else a for a in (first, second))
        stat[n] = jnp.where(in_first, one, jnp.where(in_second, two, 0.0))
    lax.fori_loop(1, n_i, push_stat, 0)
    stat_in[me_i] = stat[sample(me_i)]

    tag_wait = waiter(tag_in.at[pl.ds(0, n_i - 1)], tag_send, tag_recv)
    tag_wait.wait_recv()
    part_waits = [
        waiter(part_in.at[k, pl.ds(0, n_i - 1)], part_send.at[k], part_recv.at[k])
        for k in range(kv_local)
    ]
    stat_wait = waiter(stat_in.at[pl.ds(0, n_i - 1)], stat_send, stat_recv)

    def side_by_side(ref):
        groups = [functools.reduce(jnp.add, [ref[g * 8 + n] for n in range(8)]) for g in range(n_i // 8)]
        return jnp.concatenate(groups, axis=1)

    key = iota((1, n_i * 16), 1)
    row = iota((n_x * 8, 1), 0)
    prompt = (row // 8 * 2 + lax.rem(me_i // SAMPLES, 2)).astype(f32)
    same = (lax.rem(key, 8) == lax.rem(row, 8)) & (side_by_side(tag_in)[:1] == prompt)
    stat_wait.wait_recv()
    st = side_by_side(stat_in)
    tile = jnp.zeros((n_x * 8, 128), f32)
    for k in range(kv_local):
        part_waits[k].wait_recv()
        peaks = jnp.where(same, st[k * 2 : k * 2 + 1], masked_score)
        peak = jnp.max(peaks, axis=1, keepdims=True)
        factor = jnp.where(same, jnp.exp2((peaks - peak) * exponent), 0.0)
        mass = jnp.sum(factor * st[k * 2 + 1 : k * 2 + 2], axis=1, keepdims=True)
        high = factor.astype(bf16)
        low = (factor - high.astype(f32)).astype(bf16)
        parts = part_in[k].reshape(n_i * 16, 128)
        total = lax.dot_general(high, parts, NN, preferred_element_type=f32)
        total = total + lax.dot_general(low, parts, NN, preferred_element_type=f32)
        fin[:, k * 8 : k * 8 + 8] = total.reshape(n_x, 8, 128)
        tile = jnp.where(lane == k * 2, peak, jnp.where(lane == k * 2 + 1, mass, tile))
    fin[:, kv_local * 8 : kv_local * 8 + 8] = tile.reshape(n_x, 8, 128)
    for d in range(1, n_x):
        x = mate(d)
        push(fin.at[x], fin_in.at[me_x], fin_send, fin_recv, (x, me_i))
    fin_in[me_x] = fin[me_x]
    fin_wait = waiter(fin_in.at[pl.ds(0, n_x - 1)], fin_send, fin_recv)
    fin_wait.wait_recv()

    for g in range(n_x):
        st = fin_in[g, kv_local * 8 : kv_local * 8 + 8]
        for k in range(kv_local):
            at = (g * kv_local + k) * 8
            span = slice(at, at + 8)
            prefix_peak = st[:, k * 2 : k * 2 + 1]
            prefix_mass = st[:, k * 2 + 1 : k * 2 + 2]
            peak = own_m[span, :]
            top = jnp.maximum(prefix_peak, peak)
            from_prefix = jnp.exp2((prefix_peak - top) * exponent)
            from_own = jnp.exp2((peak - top) * exponent)
            numer = from_prefix * fin_in[g, k * 8 : k * 8 + 8] + from_own * own_acc[span, :]
            denom = from_prefix * prefix_mass + from_own * own_l[span, :]
            result = (numer / denom).astype(bf16)
            for n in range(2):
                head = (g * kv_local + k) * 2 + n
                out_ref[:, head * 128 : head * 128 + 128] = result[n * 4 : n * 4 + 4]

    for pair in range(pairs):
        for dx in range(n_x):
            q_wait(pair, dx).wait_send()
            waiter(
                q_all.at[pair, me_c, 0], forward_send.at[pair, dx], forward_recv.at[pair, dx]
            ).wait_send()
    for k in range(kv_local):
        part_waits[k].wait_send()
    tag_wait.wait_send()
    stat_wait.wait_send()
    fin_wait.wait_send()


def local(
    n_x,
    n_i,
    queries,
    new_kv,
    suffix_kv,
    suffix_len,
    prefix_len,
    prefix_kv,
    block_prompt,
    block_index,
    block_count,
):
    steps, rows_dev, heads, width = queries.shape
    slots, kv_local, block_len = prefix_kv.shape[1:4]
    rows = steps * heads
    n_j = n_i // 2
    q = queries.reshape(rows, width)
    new = new_kv.reshape(2, -1, width)
    suffix = suffix_kv.reshape(2, -1, width)
    keys = suffix.shape[1]
    chunk = 1024
    ints = (block_prompt, block_index, block_count, prefix_len, suffix_len)
    hbm = pl.BlockSpec(memory_space=pl.ANY)
    dma = pltpu.SemaphoreType.DMA
    per_row = pltpu.VMEM((rows, width), f32)
    out = pl.pallas_call(
        functools.partial(kernel, n_x, n_i, block_len, slots),
        out_shape=jax.ShapeDtypeStruct((steps, heads * width), bf16),
        in_specs=[hbm] * 9,
        out_specs=pl.BlockSpec(memory_space=pltpu.VMEM),
        scratch_shapes=[pltpu.SMEM(a.shape, a.dtype) for a in ints]
        + [
            pltpu.VMEM(q.shape, bf16),
            pltpu.VMEM(new.shape, bf16),
            pltpu.VMEM((kv_local, 2, slots, block_len, width), bf16),
            pltpu.VMEM((2, keys, width), bf16),
            pltpu.VMEM((n_x, kv_local // 2, 16, width), bf16),
            pltpu.VMEM((kv_local // 2, 2, n_x, n_j, 16, width), bf16),
            pltpu.VMEM((2, 8, rows, width), bf16),
            pltpu.VMEM((keys // chunk, rows, chunk), f32),
            per_row,
            per_row,
            per_row,
            pltpu.VMEM((3, rows, width), f32),
            per_row,
            pltpu.VMEM((8, 128), f32),
            pltpu.VMEM((n_i, 8, 128), f32),
            pltpu.VMEM((kv_local, SAMPLES, 16, width), bf16),
            pltpu.VMEM((kv_local, n_i, 16, width), bf16),
            pltpu.VMEM((SAMPLES, 8, 128), f32),
            pltpu.VMEM((n_i, 8, 128), f32),
            pltpu.VMEM((n_x, (kv_local + 1) * 8, width), f32),
            pltpu.VMEM((n_x, (kv_local + 1) * 8, width), f32),
            dma((len(ints),)),
            dma((2,)),
            dma((kv_local,)),
            dma,
            dma((kv_local // 2, n_x)),
            dma((kv_local // 2, n_x)),
            dma((kv_local // 2, n_x)),
            dma((kv_local // 2, n_x)),
            dma,
            dma,
            dma((kv_local,)),
            dma((kv_local,)),
            dma,
            dma,
            dma,
            dma,
        ],
        compiler_params=pltpu.CompilerParams(
            collective_id=0, has_side_effects=True, vmem_limit_bytes=60 << 20
        ),
        name="decode_attention",
    )(*ints, q, new, suffix, prefix_kv)
    return out.reshape(steps, rows_dev, heads * width)


def solution(mesh):
    return jax.shard_map(
        functools.partial(local, mesh.shape["rows"], mesh.shape["prefix"]),
        mesh=mesh,
        in_specs=(
            P(None, ("rows", "prefix"), None, None),
            P(None, None, ("rows", "prefix"), None, None),
            P(None, ("rows", "prefix"), None, None, None),
            P(("rows", "prefix")),
            P(),
            P(None, "prefix", "rows", None, None),
            P("prefix", None),
            P("prefix", None),
            P("prefix"),
        ),
        out_specs=P(None, ("rows", "prefix"), None),
        check_vma=False,
    )
```

```python
import functools
import math

import jax
import jax.numpy as jnp
from jax import lax
from jax.experimental import pallas as pl
from jax.experimental.pallas import tpu as pltpu
from jax.sharding import PartitionSpec as P

MESH = pl.DeviceIdType.MESH
SAMPLES = 16
masked_score = -1e30
exponent = 168.0 ** (-0.5) * math.log2(math.e)
f32 = jnp.float32
bf16 = jnp.bfloat16
NT = (((1,), (1,)), ((), ()))
NN = (((1,), (0,)), ((), ()))
X_ORDER = (0, 1, 3, 2)


def iota(shape, dim):
    return lax.broadcasted_iota(jnp.int32, shape, dim)


def kernel(
    n_x,
    n_i,
    block_len,
    slots,
    prompt_hbm,
    index_hbm,
    count_hbm,
    prefix_len_hbm,
    suffix_len_hbm,
    q_hbm,
    new_hbm,
    suffix_hbm,
    prefix_hbm,
    out_ref,
    prompt_ref,
    index_ref,
    count_ref,
    prefix_len_ref,
    suffix_len_ref,
    q_ref,
    new_ref,
    kv,
    suf,
    q_own,
    q_all,
    q_prompt,
    own_s,
    own_acc,
    own_m,
    own_l,
    m_sel,
    packed,
    tag,
    tag_in,
    part,
    part_in,
    stat,
    stat_in,
    last_stat,
    last_stat_in,
    fin,
    fin_in,
    last_fin,
    last_fin_in,
    int_sem,
    small_sem,
    kv_sem,
    suf_sem,
    q_send,
    q_recv,
    forward_send,
    forward_recv,
    tag_send,
    tag_recv,
    part_send,
    part_recv,
    stat_send,
    stat_recv,
    last_stat_send,
    last_stat_recv,
    fin_send,
    fin_recv,
    last_fin_send,
    last_fin_recv,
):
    me_x = lax.axis_index("rows")
    me_i = lax.axis_index("prefix")
    me_j = me_i // 2
    me_c = lax.rem(me_i, 2)
    other_c = 1 - me_c
    sibling = (me_x, me_j * 2 + other_c)
    n_j = n_i // 2
    kv_local = kv.shape[0]
    rows = q_ref.shape[0]
    half_j = SAMPLES // 2
    lane = iota((1, 128), 1)
    pairs = kv_local // 2

    def peer(d):
        to = me_i + d
        return jnp.where(to >= n_i, to - n_i, to)

    me_sample = lax.rem(me_i, SAMPLES)

    def sample(d):
        n = me_sample + d % SAMPLES
        return jnp.where(n >= SAMPLES, n - SAMPLES, n)

    def on_core(d):
        return lax.rem(me_j + d, n_j) * 2 + me_c

    def mate(d):
        return lax.rem(me_x + d, n_x)

    barrier = pltpu.get_barrier_semaphore()

    def greet_other(j, carry):
        pl.semaphore_signal(
            barrier, inc=1, device_id=(me_x, j * 2 + other_c), device_id_type=MESH
        )
        return carry

    lax.fori_loop(0, n_j, greet_other, 0)
    for dx in range(n_x):

        def greet(d, carry, dx=dx):
            pl.semaphore_signal(
                barrier, inc=1, device_id=(mate(dx), on_core(d)), device_id_type=MESH
            )
            return carry

        lax.fori_loop(1 if dx == 0 else 0, n_j, greet, 0)

    small_copies = [
        pltpu.make_async_copy(q_hbm, q_ref, small_sem.at[0]),
        pltpu.make_async_copy(new_hbm, new_ref, small_sem.at[1]),
    ]
    int_copies = [
        pltpu.make_async_copy(src, dst, int_sem.at[n])
        for n, (src, dst) in enumerate(
            (
                (prompt_hbm, prompt_ref),
                (index_hbm, index_ref),
                (count_hbm, count_ref),
                (prefix_len_hbm, prefix_len_ref),
                (suffix_len_hbm, suffix_len_ref),
            )
        )
    ]
    suf_copy = pltpu.make_async_copy(suffix_hbm, suf, suf_sem)
    kv_copies = [
        pltpu.make_async_copy(prefix_hbm.at[:, :, k], kv.at[k], kv_sem.at[k])
        for k in range(kv_local)
    ]
    for copy in small_copies + int_copies + [suf_copy]:
        copy.start()

    r = iota((rows, rows), 0)
    c = iota((rows, rows), 1)
    source = lax.rem(r, 4) * 32 + (r // 8) * 2 + lax.rem(r // 4, 2)
    order = jnp.where(c == source, 1.0, 0.0).astype(bf16)
    small_copies[0].wait()
    q_mine = lax.dot_general(order, q_ref[...], NN, preferred_element_type=f32).astype(bf16)
    q_own[...] = q_mine.reshape(n_x, pairs, 16, 128)
    for pair in range(pairs):
        q_all[pair, me_c, me_x, me_j] = q_own[me_x, pair]
    packed[...] = jnp.zeros_like(packed)

    pl.semaphore_wait(barrier, n_x * n_j - 1 + n_j)

    def waiter(ref, send, recv):
        return pltpu.make_async_remote_copy(
            src_ref=ref,
            dst_ref=ref,
            send_sem=send,
            recv_sem=recv,
            device_id=sibling,
            device_id_type=MESH,
        )

    def push(src, dst, send, recv, to):
        pltpu.make_async_remote_copy(
            src_ref=src,
            dst_ref=dst,
            send_sem=send,
            recv_sem=recv,
            device_id=to,
            device_id_type=MESH,
        ).start()

    for pair in range(pairs):
        for dx in X_ORDER:

            def push_q(d, carry, pair=pair, dx=dx):
                x = mate(dx)
                push(
                    q_own.at[x, pair],
                    q_all.at[pair, me_c, me_x, me_j],
                    q_send.at[pair, dx],
                    q_recv.at[pair, dx],
                    (x, on_core(d)),
                )
                return carry

            lax.fori_loop(1 if dx == 0 else 0, n_j, push_q, 0)
    for copy in kv_copies:
        copy.start()

    def q_wait(pair, dx):
        chunks = q_all.at[pair, me_c, 0, pl.ds(0, n_j - 1 if dx == 0 else n_j)]
        return waiter(chunks, q_send.at[pair, dx], q_recv.at[pair, dx])

    for copy in small_copies[1:] + int_copies + [suf_copy]:
        copy.wait()
    count = count_ref[0]
    prompt_a = prompt_ref[0, 0]
    prompt_b = prompt_ref[0, jnp.maximum(count - 1, 0)]
    base = lax.rem(me_i, 8) * 16
    in_first = (lane >= base) & (lane < base + 8)
    in_second = (lane >= base + 8) & (lane < base + 16)
    tag_a = prompt_a.astype(f32)
    tag_b = jnp.where(prompt_b == prompt_a, -1, prompt_b).astype(f32)
    tags = jnp.where(in_first, tag_a, jnp.where(in_second, tag_b, 0.0))
    tag[...] = jnp.broadcast_to(tags, (8, 128))
    tag_in[me_i] = tag[...]

    def push_tag(d, carry):
        push(tag, tag_in.at[me_i], tag_send, tag_recv, (me_x, peer(d)))
        return carry

    lax.fori_loop(1, n_i, push_tag, 0)
    chunk = own_s.shape[2]
    chunks = own_s.shape[0]
    suffix_len = suffix_len_ref[0]
    row_head = iota((rows, 1), 0) // 8
    row_step = lax.rem(iota((rows, 1), 0), 4)
    near = lax.dot_general(q_mine, new_ref[0], NT, preferred_element_type=f32)
    key = iota((1, near.shape[1]), 1)
    near_live = (lax.rem(key, 16) == row_head) & (key // 16 <= row_step)
    near = jnp.where(near_live, near, masked_score)
    key = iota((1, chunk), 1)
    same_head = lax.rem(key, 16) == row_head

    def far_scores(n, peak):
        s = lax.dot_general(
            q_mine, suf[0, pl.ds(n * chunk, chunk)], NT, preferred_element_type=f32
        )
        live = same_head & (n * (chunk // 16) + key // 16 < suffix_len)
        s = jnp.where(live, s, masked_score)
        own_s[n] = s
        return jnp.maximum(peak, jnp.max(s, axis=1, keepdims=True))

    own_peak = lax.fori_loop(0, chunks, far_scores, jnp.max(near, axis=1, keepdims=True))
    near_w = jnp.exp2((near - own_peak) * exponent).astype(bf16)
    near_sum = lax.dot_general(near_w, new_ref[1], NN, preferred_element_type=f32)
    near_mass = jnp.sum(near_w.astype(f32), axis=1, keepdims=True)
    ones = jnp.ones((chunk, 128), bf16)

    def far_sums(n, carry):
        total, mass = carry
        w = jnp.exp2((own_s[n] - own_peak) * exponent).astype(bf16)
        values = jnp.concatenate([suf[1, pl.ds(n * chunk, chunk)], ones], axis=1)
        both = lax.dot_general(w, values, NN, preferred_element_type=f32)
        return total + both[:, :128], mass + both[:, 128:]

    total, mass = lax.fori_loop(
        0, chunks, far_sums, (near_sum, jnp.broadcast_to(near_mass, (rows, 128)))
    )
    own_acc[...] = total
    own_l[...] = mass
    own_m[...] = jnp.broadcast_to(own_peak, (rows, 128))

    column = iota((1, block_len), 1)
    ones = jnp.ones((block_len, 128), bf16)
    in_a = [jnp.where(prompt_ref[0, j] == prompt_a, 1, 0) for j in range(slots)]
    outside_a = outside_b = jnp.full((1, 128), masked_score, f32)
    for j in range(slots):
        inside = jnp.where(prompt_ref[0, j] == prompt_a, 0.0, masked_score)
        outside_a = jnp.where(lane == j, inside, outside_a)
        inside = jnp.where(prompt_ref[0, j] == prompt_b, 0.0, masked_score)
        outside_b = jnp.where(lane == j, inside, outside_b)

    def forward_q(pair):
        for dx in X_ORDER:
            q_wait(pair, dx).wait_recv()
            mine = q_all.at[pair, me_c, lax.rem(me_x + n_x - dx, n_x)]
            push(mine, mine, forward_send.at[pair, dx], forward_recv.at[pair, dx], sibling)

    def push_part(k):
        for d in range(1, n_i):
            push(
                part.at[k, sample(d)],
                part_in.at[k, me_i],
                part_send.at[k],
                part_recv.at[k],
                (me_x, peer(d)),
            )
        part_in[k, me_i] = part[k, me_sample]

    def push_stats(last):
        here, there = (last_stat, last_stat_in) if last else (stat, stat_in)
        send, recv = (last_stat_send, last_stat_recv) if last else (stat_send, stat_recv)
        turned = packed[...].T
        first = pltpu.roll(turned[:8], base, 1)
        second = pltpu.roll(turned[8:16], base + 8, 1)
        for n in range(SAMPLES):
            shift = (128 - 8 * n) % 128
            one, two = (pltpu.roll(a, shift, 1) if shift else a for a in (first, second))
            both = jnp.where(in_first, one, jnp.where(in_second, two, 0.0))
            here[n] = both[6:8] if last else both

        for d in range(1, n_i):
            push(here.at[sample(d)], there.at[me_i], send, recv, (me_x, peer(d)))
        there[me_i] = here[me_sample]

    forward_q(0)
    for k in range(kv_local):
        pair = k // 2
        if k % 2 == 0:
            for dx in X_ORDER:
                waiter(
                    q_all.at[pair, me_c, 0], forward_send.at[pair, dx], forward_recv.at[pair, dx]
                ).wait_recv()
            for half in range(2):
                for x in range(n_x):
                    v = q_all[pair, :, x, pl.ds(half * half_j, half_j)].astype(f32)
                    v = v.swapaxes(0, 1).reshape(SAMPLES, 2, 8, 128)
                    for n in range(2):
                        q_prompt[n, 2 * x + half] = v[:, n].reshape(rows, 128).astype(bf16)
        elif pair + 1 < pairs:
            forward_q(pair + 1)
        kv_copies[k].wait()

        accs, ms = [], []
        peaks = jnp.full((rows, 128), masked_score, f32)
        masses = jnp.zeros((rows, 128), f32)
        for j in range(slots):
            prompt = prompt_ref[0, j]
            live = prefix_len_ref[prompt] - index_ref[0, j] * block_len
            live = jnp.where(j < count, live, 0)
            s = lax.dot_general(
                q_prompt[k % 2, prompt], kv[k, 0, j], NT, preferred_element_type=f32
            )
            s = jnp.where(column < live, s, masked_score)
            m = jnp.max(s, axis=1, keepdims=True)
            w = jnp.exp2((s - m) * exponent).astype(bf16)
            values = jnp.concatenate([kv[k, 1, j], ones], axis=1)
            both = lax.dot_general(w, values, NN, preferred_element_type=f32)
            accs.append(both[:, :128])
            ms.append(m)
            peaks = jnp.where(lane == j, m, peaks)
            masses = jnp.where(lane == j, both[:, 128:], masses)

        pack = packed[...]
        for place, outside in ((1, outside_a), (2, outside_b)):
            shifted = peaks + outside
            peak = jnp.max(shifted, axis=1, keepdims=True)
            take = jnp.exp2((shifted - peak) * exponent)
            mass = jnp.sum(take * masses, axis=1, keepdims=True)
            m_sel[place] = jnp.broadcast_to(peak, (rows, 128))
            at = (place - 1) * 8 + k * 2
            pack = jnp.where(lane == at, peak, jnp.where(lane == at + 1, mass, pack))
        packed[...] = pack
        total_a = total_b = jnp.zeros((rows, 128), f32)
        for j in range(slots):
            take = jnp.exp2((ms[j] - m_sel[2 - in_a[j]]) * exponent)
            taken = take * accs[j]
            total_a = total_a + jnp.where(in_a[j] == 1, taken, 0.0)
            total_b = total_b + jnp.where(in_a[j] == 1, 0.0, taken)
        parts = [t.reshape(SAMPLES, 8, 128) for t in (total_a, total_b)]
        part[k] = jnp.concatenate(parts, axis=1).astype(bf16)
        push_part(k)
        if k >= kv_local - 2:
            push_stats(k == kv_local - 1)

    tag_wait = waiter(tag_in.at[pl.ds(0, n_i - 1)], tag_send, tag_recv)
    tag_wait.wait_recv()
    part_waits = [
        waiter(part_in.at[k, pl.ds(0, n_i - 1)], part_send.at[k], part_recv.at[k])
        for k in range(kv_local)
    ]
    stat_wait = waiter(stat_in.at[pl.ds(0, n_i - 1)], stat_send, stat_recv)
    last_stat_wait = waiter(
        last_stat_in.at[pl.ds(0, n_i - 1)], last_stat_send, last_stat_recv
    )

    def side_by_side(ref):
        groups = [functools.reduce(jnp.add, [ref[g * 8 + n] for n in range(8)]) for g in range(n_i // 8)]
        return jnp.concatenate(groups, axis=1)

    key = iota((1, n_i * 16), 1)
    row = iota((n_x * 8, 1), 0)
    prompt = (row // 8 * 2 + lax.rem(me_i // SAMPLES, 2)).astype(f32)
    same = (lax.rem(key, 8) == lax.rem(row, 8)) & (side_by_side(tag_in)[:1] == prompt)

    def combine(k, st):
        part_waits[k].wait_recv()
        peaks = jnp.where(same, st[:1], masked_score)
        peak = jnp.max(peaks, axis=1, keepdims=True)
        factor = jnp.where(same, jnp.exp2((peaks - peak) * exponent), 0.0)
        mass = jnp.sum(factor * st[1:], axis=1, keepdims=True)
        high = factor.astype(bf16)
        low = (factor - high.astype(f32)).astype(bf16)
        parts = part_in[k].reshape(n_i * 16, 128)
        total = lax.dot_general(high, parts, NN, preferred_element_type=f32)
        total = total + lax.dot_general(low, parts, NN, preferred_element_type=f32)
        return total.reshape(n_x, 8, 128), peak, mass

    def push_fin(here, there, send, recv):
        for d in range(1, n_x):
            x = mate(d)
            push(here.at[x], there.at[me_x], send, recv, (x, me_i))
        there[me_x] = here[me_x]
        return waiter(there.at[pl.ds(0, n_x - 1)], send, recv)

    def finish(g, k, total, st, at):
        span = pl.ds((g * kv_local + k) * 8, 8)
        prefix_peak = st[:, at : at + 1]
        prefix_mass = st[:, at + 1 : at + 2]
        peak = own_m[span, :]
        top = jnp.maximum(prefix_peak, peak)
        from_prefix = jnp.exp2((prefix_peak - top) * exponent)
        from_own = jnp.exp2((peak - top) * exponent)
        numer = from_prefix * total + from_own * own_acc[span, :]
        denom = from_prefix * prefix_mass + from_own * own_l[span, :]
        result = (numer / denom).astype(bf16)
        for n in range(2):
            head = (g * kv_local + k) * 2 + n
            out_ref[:, head * 128 : head * 128 + 128] = result[n * 4 : n * 4 + 4]

    early = kv_local - 1
    stat_wait.wait_recv()
    st = side_by_side(stat_in)
    tile = jnp.zeros((n_x * 8, 128), f32)
    for k in range(early):
        total, peak, mass = combine(k, st[k * 2 : k * 2 + 2])
        fin[:, k * 8 : k * 8 + 8] = total
        tile = jnp.where(lane == k * 2, peak, jnp.where(lane == k * 2 + 1, mass, tile))
    fin[:, early * 8 : early * 8 + 8] = tile.reshape(n_x, 8, 128)
    fin_wait = push_fin(fin, fin_in, fin_send, fin_recv)

    last_stat_wait.wait_recv()
    total, peak, mass = combine(early, side_by_side(last_stat_in))
    last_fin[:, :8] = total
    tile = jnp.where(lane == 0, peak, jnp.where(lane == 1, mass, 0.0))
    last_fin[:, 8:16] = tile.reshape(n_x, 8, 128)
    last_fin_wait = push_fin(last_fin, last_fin_in, last_fin_send, last_fin_recv)

    fin_wait.wait_recv()
    for g in range(n_x):
        st = fin_in[g, early * 8 : early * 8 + 8]
        for k in range(early):
            finish(g, k, fin_in[g, k * 8 : k * 8 + 8], st, k * 2)
    last_fin_wait.wait_recv()
    for g in range(n_x):
        finish(g, early, last_fin_in[g, :8], last_fin_in[g, 8:16], 0)

    for pair in range(pairs):
        for dx in range(n_x):
            q_wait(pair, dx).wait_send()
            waiter(
                q_all.at[pair, me_c, 0], forward_send.at[pair, dx], forward_recv.at[pair, dx]
            ).wait_send()
    for k in range(kv_local):
        part_waits[k].wait_send()
    tag_wait.wait_send()
    stat_wait.wait_send()
    last_stat_wait.wait_send()
    fin_wait.wait_send()
    last_fin_wait.wait_send()


def local(
    n_x,
    n_i,
    queries,
    new_kv,
    suffix_kv,
    suffix_len,
    prefix_len,
    prefix_kv,
    block_prompt,
    block_index,
    block_count,
):
    steps, rows_dev, heads, width = queries.shape
    slots, kv_local, block_len = prefix_kv.shape[1:4]
    rows = steps * heads
    n_j = n_i // 2
    q = queries.reshape(rows, width)
    new = new_kv.reshape(2, -1, width)
    suffix = suffix_kv.reshape(2, -1, width)
    keys = suffix.shape[1]
    chunk = 1024
    ints = (block_prompt, block_index, block_count, prefix_len, suffix_len)
    hbm = pl.BlockSpec(memory_space=pl.ANY)
    dma = pltpu.SemaphoreType.DMA
    per_row = pltpu.VMEM((rows, width), f32)
    out = pl.pallas_call(
        functools.partial(kernel, n_x, n_i, block_len, slots),
        out_shape=jax.ShapeDtypeStruct((steps, heads * width), bf16),
        in_specs=[hbm] * 9,
        out_specs=pl.BlockSpec(memory_space=pltpu.VMEM),
        scratch_shapes=[pltpu.SMEM(a.shape, a.dtype) for a in ints]
        + [
            pltpu.VMEM(q.shape, bf16),
            pltpu.VMEM(new.shape, bf16),
            pltpu.VMEM((kv_local, 2, slots, block_len, width), bf16),
            pltpu.VMEM((2, keys, width), bf16),
            pltpu.VMEM((n_x, kv_local // 2, 16, width), bf16),
            pltpu.VMEM((kv_local // 2, 2, n_x, n_j, 16, width), bf16),
            pltpu.VMEM((2, 8, rows, width), bf16),
            pltpu.VMEM((keys // chunk, rows, chunk), f32),
            per_row,
            per_row,
            per_row,
            pltpu.VMEM((3, rows, width), f32),
            per_row,
            pltpu.VMEM((8, 128), f32),
            pltpu.VMEM((n_i, 8, 128), f32),
            pltpu.VMEM((kv_local, SAMPLES, 16, width), bf16),
            pltpu.VMEM((kv_local, n_i, 16, width), bf16),
            pltpu.VMEM((SAMPLES, 8, 128), f32),
            pltpu.VMEM((n_i, 8, 128), f32),
            pltpu.VMEM((SAMPLES, 2, 128), f32),
            pltpu.VMEM((n_i, 2, 128), f32),
            pltpu.VMEM((n_x, kv_local * 8, width), f32),
            pltpu.VMEM((n_x, kv_local * 8, width), f32),
            pltpu.VMEM((n_x, 16, width), f32),
            pltpu.VMEM((n_x, 16, width), f32),
            dma((len(ints),)),
            dma((2,)),
            dma((kv_local,)),
            dma,
            dma((kv_local // 2, n_x)),
            dma((kv_local // 2, n_x)),
            dma((kv_local // 2, n_x)),
            dma((kv_local // 2, n_x)),
            dma,
            dma,
            dma((kv_local,)),
            dma((kv_local,)),
            dma,
            dma,
            dma,
            dma,
            dma,
            dma,
            dma,
            dma,
        ],
        compiler_params=pltpu.CompilerParams(
            collective_id=0, has_side_effects=True, vmem_limit_bytes=60 << 20
        ),
        name="decode_attention",
    )(*ints, q, new, suffix, prefix_kv)
    return out.reshape(steps, rows_dev, heads * width)


def solution(mesh):
    return jax.shard_map(
        functools.partial(local, mesh.shape["rows"], mesh.shape["prefix"]),
        mesh=mesh,
        in_specs=(
            P(None, ("rows", "prefix"), None, None),
            P(None, None, ("rows", "prefix"), None, None),
            P(None, ("rows", "prefix"), None, None, None),
            P(("rows", "prefix")),
            P(),
            P(None, "prefix", "rows", None, None),
            P("prefix", None),
            P("prefix", None),
            P("prefix"),
        ),
        out_specs=P(None, ("rows", "prefix"), None),
        check_vma=False,
    )
```

```python
import functools
import math

import jax
import jax.numpy as jnp
from jax import lax
from jax.experimental import pallas as pl
from jax.experimental.pallas import tpu as pltpu
from jax.sharding import PartitionSpec as P

MESH = pl.DeviceIdType.MESH
SAMPLES = 16
masked_score = -1e30
exponent = 168.0 ** (-0.5) * math.log2(math.e)
f32 = jnp.float32
bf16 = jnp.bfloat16
NT = (((1,), (1,)), ((), ()))
NN = (((1,), (0,)), ((), ()))
X_ORDER = (0, 1, 3, 2)


def iota(shape, dim):
    return lax.broadcasted_iota(jnp.int32, shape, dim)


def kernel(
    n_x,
    n_i,
    block_len,
    slots,
    prompt_hbm,
    index_hbm,
    count_hbm,
    prefix_len_hbm,
    suffix_len_hbm,
    q_hbm,
    new_hbm,
    suffix_hbm,
    prefix_hbm,
    out_ref,
    prompt_ref,
    index_ref,
    count_ref,
    prefix_len_ref,
    suffix_len_ref,
    q_ref,
    new_ref,
    kv,
    suf,
    q_own,
    q_all,
    q_prompt,
    own_s,
    own_acc,
    own_m,
    own_l,
    m_sel,
    packed,
    tag,
    tag_in,
    part,
    part_in,
    stat,
    stat_in,
    last_stat,
    last_stat_in,
    fin,
    fin_in,
    last_fin,
    last_fin_in,
    int_sem,
    small_sem,
    kv_sem,
    suf_sem,
    q_send,
    q_recv,
    forward_send,
    forward_recv,
    tag_send,
    tag_recv,
    part_send,
    part_recv,
    stat_send,
    stat_recv,
    last_stat_send,
    last_stat_recv,
    fin_send,
    fin_recv,
    last_fin_send,
    last_fin_recv,
):
    me_x = lax.axis_index("rows")
    me_i = lax.axis_index("prefix")
    me_j = me_i // 2
    me_c = lax.rem(me_i, 2)
    other_c = 1 - me_c
    sibling = (me_x, me_j * 2 + other_c)
    n_j = n_i // 2
    kv_local = kv.shape[0]
    rows = q_ref.shape[0]
    half_j = SAMPLES // 2
    lane = iota((1, 128), 1)
    pairs = kv_local // 2

    def peer(d):
        to = me_i + d
        return jnp.where(to >= n_i, to - n_i, to)

    me_sample = lax.rem(me_i, SAMPLES)

    def sample(d):
        n = me_sample + d % SAMPLES
        return jnp.where(n >= SAMPLES, n - SAMPLES, n)

    def on_core(d):
        to = me_i + 2 * d
        return jnp.where(to >= n_i, to - n_i, to)

    def mate(d):
        to = me_x + d
        return jnp.where(to >= n_x, to - n_x, to)

    barrier = pltpu.get_barrier_semaphore()
    for j in range(n_j):
        pl.semaphore_signal(
            barrier, inc=1, device_id=(me_x, j * 2 + other_c), device_id_type=MESH
        )
    for dx in range(n_x):

        for d in range(1 if dx == 0 else 0, n_j):
            pl.semaphore_signal(
                barrier, inc=1, device_id=(mate(dx), on_core(d)), device_id_type=MESH
            )

    small_copies = [
        pltpu.make_async_copy(q_hbm, q_ref, small_sem.at[0]),
        pltpu.make_async_copy(new_hbm, new_ref, small_sem.at[1]),
    ]
    int_copies = [
        pltpu.make_async_copy(src, dst, int_sem.at[n])
        for n, (src, dst) in enumerate(
            (
                (prompt_hbm, prompt_ref),
                (index_hbm, index_ref),
                (count_hbm, count_ref),
                (prefix_len_hbm, prefix_len_ref),
                (suffix_len_hbm, suffix_len_ref),
            )
        )
    ]
    suf_copy = pltpu.make_async_copy(suffix_hbm, suf, suf_sem)
    kv_copies = [
        pltpu.make_async_copy(prefix_hbm.at[:, :, k], kv.at[k], kv_sem.at[k])
        for k in range(kv_local)
    ]
    for copy in small_copies + int_copies + [suf_copy]:
        copy.start()

    r = iota((rows, rows), 0)
    c = iota((rows, rows), 1)
    source = lax.rem(r, 4) * 32 + (r // 8) * 2 + lax.rem(r // 4, 2)
    order = jnp.where(c == source, 1.0, 0.0).astype(bf16)
    small_copies[0].wait()
    q_mine = lax.dot_general(order, q_ref[...], NN, preferred_element_type=f32).astype(bf16)
    q_own[...] = q_mine.reshape(n_x, pairs, 16, 128)
    for pair in range(pairs):
        q_all[pair, me_c, me_x, me_j] = q_own[me_x, pair]
    packed[...] = jnp.zeros_like(packed)

    pl.semaphore_wait(barrier, n_x * n_j - 1 + n_j)

    def waiter(ref, send, recv):
        return pltpu.make_async_remote_copy(
            src_ref=ref,
            dst_ref=ref,
            send_sem=send,
            recv_sem=recv,
            device_id=sibling,
            device_id_type=MESH,
        )

    def push(src, dst, send, recv, to):
        pltpu.make_async_remote_copy(
            src_ref=src,
            dst_ref=dst,
            send_sem=send,
            recv_sem=recv,
            device_id=to,
            device_id_type=MESH,
        ).start()

    def push_pair(pair):
        for dx in X_ORDER:
            x = mate(dx)
            for d in range(1 if dx == 0 else 0, n_j):
                push(
                    q_own.at[x, pair],
                    q_all.at[pair, me_c, me_x, me_j],
                    q_send.at[pair, dx],
                    q_recv.at[pair, dx],
                    (x, on_core(d)),
                )

    push_pair(0)
    for copy in kv_copies:
        copy.start()

    def q_wait(pair, dx):
        chunks = q_all.at[pair, me_c, 0, pl.ds(0, n_j - 1 if dx == 0 else n_j)]
        return waiter(chunks, q_send.at[pair, dx], q_recv.at[pair, dx])

    for copy in small_copies[1:] + int_copies + [suf_copy]:
        copy.wait()
    count = count_ref[0]
    prompt_a = prompt_ref[0, 0]
    prompt_b = prompt_ref[0, jnp.maximum(count - 1, 0)]
    base = lax.rem(me_i, 8) * 16
    in_first = (lane >= base) & (lane < base + 8)
    in_second = (lane >= base + 8) & (lane < base + 16)
    tag_a = prompt_a.astype(f32)
    tag_b = jnp.where(prompt_b == prompt_a, -1, prompt_b).astype(f32)
    tags = jnp.where(in_first, tag_a, jnp.where(in_second, tag_b, 0.0))
    tag[...] = jnp.broadcast_to(tags, (8, 128))
    tag_in[me_i] = tag[...]

    chunk = own_s.shape[2]
    chunks = own_s.shape[0]
    suffix_len = suffix_len_ref[0]
    row_head = iota((rows, 1), 0) // 8
    row_step = lax.rem(iota((rows, 1), 0), 4)
    near = lax.dot_general(q_mine, new_ref[0], NT, preferred_element_type=f32)
    key = iota((1, near.shape[1]), 1)
    near_live = (lax.rem(key, 16) == row_head) & (key // 16 <= row_step)
    near = jnp.where(near_live, near, masked_score)
    key = iota((1, chunk), 1)
    same_head = lax.rem(key, 16) == row_head

    def far_scores(n, peak):
        s = lax.dot_general(
            q_mine, suf[0, pl.ds(n * chunk, chunk)], NT, preferred_element_type=f32
        )
        live = same_head & (n * (chunk // 16) + key // 16 < suffix_len)
        s = jnp.where(live, s, masked_score)
        own_s[n] = s
        return jnp.maximum(peak, jnp.max(s, axis=1, keepdims=True))

    own_peak = lax.fori_loop(0, chunks, far_scores, jnp.max(near, axis=1, keepdims=True))
    near_w = jnp.exp2((near - own_peak) * exponent).astype(bf16)
    near_sum = lax.dot_general(near_w, new_ref[1], NN, preferred_element_type=f32)
    near_mass = jnp.sum(near_w.astype(f32), axis=1, keepdims=True)
    ones = jnp.ones((chunk, 128), bf16)

    def far_sums(n, carry):
        total, mass = carry
        w = jnp.exp2((own_s[n] - own_peak) * exponent).astype(bf16)
        values = jnp.concatenate([suf[1, pl.ds(n * chunk, chunk)], ones], axis=1)
        both = lax.dot_general(w, values, NN, preferred_element_type=f32)
        return total + both[:, :128], mass + both[:, 128:]

    total, mass = lax.fori_loop(
        0, chunks, far_sums, (near_sum, jnp.broadcast_to(near_mass, (rows, 128)))
    )
    own_acc[...] = total
    own_l[...] = mass
    own_m[...] = jnp.broadcast_to(own_peak, (rows, 128))

    push_pair(1)

    column = iota((1, block_len), 1)
    ones = jnp.ones((block_len, 128), bf16)
    in_a = [jnp.where(prompt_ref[0, j] == prompt_a, 1, 0) for j in range(slots)]
    outside_a = outside_b = jnp.full((1, 128), masked_score, f32)
    for j in range(slots):
        inside = jnp.where(prompt_ref[0, j] == prompt_a, 0.0, masked_score)
        outside_a = jnp.where(lane == j, inside, outside_a)
        inside = jnp.where(prompt_ref[0, j] == prompt_b, 0.0, masked_score)
        outside_b = jnp.where(lane == j, inside, outside_b)

    def forward_q(pair):
        for dx in X_ORDER:
            q_wait(pair, dx).wait_recv()
            mine = q_all.at[pair, me_c, lax.rem(me_x + n_x - dx, n_x)]
            push(mine, mine, forward_send.at[pair, dx], forward_recv.at[pair, dx], sibling)

    def push_part(k):
        for d in range(1, n_i):
            push(
                part.at[k, sample(d)],
                part_in.at[k, me_i],
                part_send.at[k],
                part_recv.at[k],
                (me_x, peer(d)),
            )
        part_in[k, me_i] = part[k, me_sample]

    def push_stats(last):
        here, there = (last_stat, last_stat_in) if last else (stat, stat_in)
        send, recv = (last_stat_send, last_stat_recv) if last else (stat_send, stat_recv)
        turned = packed[...].T
        first = pltpu.roll(turned[:8], base, 1)
        second = pltpu.roll(turned[8:16], base + 8, 1)
        for n in range(SAMPLES):
            shift = (128 - 8 * n) % 128
            one, two = (pltpu.roll(a, shift, 1) if shift else a for a in (first, second))
            both = jnp.where(in_first, one, jnp.where(in_second, two, 0.0))
            here[n] = both[6:8] if last else both

        for d in range(1, n_i):
            push(here.at[sample(d)], there.at[me_i], send, recv, (me_x, peer(d)))
        there[me_i] = here[me_sample]

    forward_q(0)
    for d in range(1, n_i):
        push(tag, tag_in.at[me_i], tag_send, tag_recv, (me_x, peer(d)))
    for k in range(kv_local):
        pair = k // 2
        if k % 2 == 0:
            for dx in X_ORDER:
                waiter(
                    q_all.at[pair, me_c, 0], forward_send.at[pair, dx], forward_recv.at[pair, dx]
                ).wait_recv()
            for half in range(2):
                for x in range(n_x):
                    v = q_all[pair, :, x, pl.ds(half * half_j, half_j)].astype(f32)
                    v = v.swapaxes(0, 1).reshape(SAMPLES, 2, 8, 128)
                    for n in range(2):
                        q_prompt[n, 2 * x + half] = v[:, n].reshape(rows, 128).astype(bf16)
        elif pair + 1 < pairs:
            forward_q(pair + 1)
        kv_copies[k].wait()

        accs, ms = [], []
        peaks = jnp.full((rows, 128), masked_score, f32)
        masses = jnp.zeros((rows, 128), f32)
        for j in range(slots):
            prompt = prompt_ref[0, j]
            live = prefix_len_ref[prompt] - index_ref[0, j] * block_len
            live = jnp.where(j < count, live, 0)
            s = lax.dot_general(
                q_prompt[k % 2, prompt], kv[k, 0, j], NT, preferred_element_type=f32
            )
            s = jnp.where(column < live, s, masked_score)
            m = jnp.max(s, axis=1, keepdims=True)
            w = jnp.exp2((s - m) * exponent).astype(bf16)
            values = jnp.concatenate([kv[k, 1, j], ones], axis=1)
            both = lax.dot_general(w, values, NN, preferred_element_type=f32)
            accs.append(both[:, :128])
            ms.append(m)
            peaks = jnp.where(lane == j, m, peaks)
            masses = jnp.where(lane == j, both[:, 128:], masses)

        pack = packed[...]
        for place, outside in ((1, outside_a), (2, outside_b)):
            shifted = peaks + outside
            peak = jnp.max(shifted, axis=1, keepdims=True)
            take = jnp.exp2((shifted - peak) * exponent)
            mass = jnp.sum(take * masses, axis=1, keepdims=True)
            m_sel[place] = jnp.broadcast_to(peak, (rows, 128))
            at = (place - 1) * 8 + k * 2
            pack = jnp.where(lane == at, peak, jnp.where(lane == at + 1, mass, pack))
        packed[...] = pack
        total_a = total_b = jnp.zeros((rows, 128), f32)
        for j in range(slots):
            take = jnp.exp2((ms[j] - m_sel[2 - in_a[j]]) * exponent)
            taken = take * accs[j]
            total_a = total_a + jnp.where(in_a[j] == 1, taken, 0.0)
            total_b = total_b + jnp.where(in_a[j] == 1, 0.0, taken)
        parts = [t.reshape(SAMPLES, 8, 128) for t in (total_a, total_b)]
        part[k] = jnp.concatenate(parts, axis=1).astype(bf16)
        push_part(k)
        if k >= kv_local - 2:
            push_stats(k == kv_local - 1)

    tag_wait = waiter(tag_in.at[pl.ds(0, n_i - 1)], tag_send, tag_recv)
    tag_wait.wait_recv()
    part_waits = [
        waiter(part_in.at[k, pl.ds(0, n_i - 1)], part_send.at[k], part_recv.at[k])
        for k in range(kv_local)
    ]
    stat_wait = waiter(stat_in.at[pl.ds(0, n_i - 1)], stat_send, stat_recv)
    last_stat_wait = waiter(
        last_stat_in.at[pl.ds(0, n_i - 1)], last_stat_send, last_stat_recv
    )

    def side_by_side(ref):
        groups = [functools.reduce(jnp.add, [ref[g * 8 + n] for n in range(8)]) for g in range(n_i // 8)]
        return jnp.concatenate(groups, axis=1)

    key = iota((1, n_i * 16), 1)
    row = iota((n_x * 8, 1), 0)
    prompt = (row // 8 * 2 + lax.rem(me_i // SAMPLES, 2)).astype(f32)
    same = (lax.rem(key, 8) == lax.rem(row, 8)) & (side_by_side(tag_in)[:1] == prompt)

    def combine(k, st):
        part_waits[k].wait_recv()
        peaks = jnp.where(same, st[:1], masked_score)
        peak = jnp.max(peaks, axis=1, keepdims=True)
        factor = jnp.where(same, jnp.exp2((peaks - peak) * exponent), 0.0)
        mass = jnp.sum(factor * st[1:], axis=1, keepdims=True)
        high = factor.astype(bf16)
        low = (factor - high.astype(f32)).astype(bf16)
        parts = part_in[k].reshape(n_i * 16, 128)
        total = lax.dot_general(high, parts, NN, preferred_element_type=f32)
        total = total + lax.dot_general(low, parts, NN, preferred_element_type=f32)
        return total.reshape(n_x, 8, 128), peak, mass

    def push_fin(here, there, send, recv):
        for d in range(1, n_x):
            x = mate(d)
            push(here.at[x], there.at[me_x], send, recv, (x, me_i))
        there[me_x] = here[me_x]
        return waiter(there.at[pl.ds(0, n_x - 1)], send, recv)

    def finish(g, k, total, st, at):
        span = pl.ds((g * kv_local + k) * 8, 8)
        prefix_peak = st[:, at : at + 1]
        prefix_mass = st[:, at + 1 : at + 2]
        peak = own_m[span, :]
        top = jnp.maximum(prefix_peak, peak)
        from_prefix = jnp.exp2((prefix_peak - top) * exponent)
        from_own = jnp.exp2((peak - top) * exponent)
        numer = from_prefix * total + from_own * own_acc[span, :]
        denom = from_prefix * prefix_mass + from_own * own_l[span, :]
        result = (numer / denom).astype(bf16)
        for n in range(2):
            head = (g * kv_local + k) * 2 + n
            out_ref[:, head * 128 : head * 128 + 128] = result[n * 4 : n * 4 + 4]

    early = kv_local - 1
    stat_wait.wait_recv()
    st = side_by_side(stat_in)
    tile = jnp.zeros((n_x * 8, 128), f32)
    for k in range(early):
        total, peak, mass = combine(k, st[k * 2 : k * 2 + 2])
        fin[:, k * 8 : k * 8 + 8] = total
        tile = jnp.where(lane == k * 2, peak, jnp.where(lane == k * 2 + 1, mass, tile))
    fin[:, early * 8 : early * 8 + 8] = tile.reshape(n_x, 8, 128)
    fin_wait = push_fin(fin, fin_in, fin_send, fin_recv)

    last_stat_wait.wait_recv()
    total, peak, mass = combine(early, side_by_side(last_stat_in))
    last_fin[:, :8] = total
    tile = jnp.where(lane == 0, peak, jnp.where(lane == 1, mass, 0.0))
    last_fin[:, 8:16] = tile.reshape(n_x, 8, 128)
    last_fin_wait = push_fin(last_fin, last_fin_in, last_fin_send, last_fin_recv)

    fin_wait.wait_recv()
    for g in range(n_x):
        st = fin_in[g, early * 8 : early * 8 + 8]
        for k in range(early):
            finish(g, k, fin_in[g, k * 8 : k * 8 + 8], st, k * 2)
    last_fin_wait.wait_recv()
    for g in range(n_x):
        finish(g, early, last_fin_in[g, :8], last_fin_in[g, 8:16], 0)

    for pair in range(pairs):
        for dx in range(n_x):
            q_wait(pair, dx).wait_send()
            waiter(
                q_all.at[pair, me_c, 0], forward_send.at[pair, dx], forward_recv.at[pair, dx]
            ).wait_send()
    for k in range(kv_local):
        part_waits[k].wait_send()
    tag_wait.wait_send()
    stat_wait.wait_send()
    last_stat_wait.wait_send()
    fin_wait.wait_send()
    last_fin_wait.wait_send()


def local(
    n_x,
    n_i,
    queries,
    new_kv,
    suffix_kv,
    suffix_len,
    prefix_len,
    prefix_kv,
    block_prompt,
    block_index,
    block_count,
):
    steps, rows_dev, heads, width = queries.shape
    slots, kv_local, block_len = prefix_kv.shape[1:4]
    rows = steps * heads
    n_j = n_i // 2
    q = queries.reshape(rows, width)
    new = new_kv.reshape(2, -1, width)
    suffix = suffix_kv.reshape(2, -1, width)
    keys = suffix.shape[1]
    chunk = 1024
    ints = (block_prompt, block_index, block_count, prefix_len, suffix_len)
    hbm = pl.BlockSpec(memory_space=pl.ANY)
    dma = pltpu.SemaphoreType.DMA
    per_row = pltpu.VMEM((rows, width), f32)
    out = pl.pallas_call(
        functools.partial(kernel, n_x, n_i, block_len, slots),
        out_shape=jax.ShapeDtypeStruct((steps, heads * width), bf16),
        in_specs=[hbm] * 9,
        out_specs=pl.BlockSpec(memory_space=pltpu.VMEM),
        scratch_shapes=[pltpu.SMEM(a.shape, a.dtype) for a in ints]
        + [
            pltpu.VMEM(q.shape, bf16),
            pltpu.VMEM(new.shape, bf16),
            pltpu.VMEM((kv_local, 2, slots, block_len, width), bf16),
            pltpu.VMEM((2, keys, width), bf16),
            pltpu.VMEM((n_x, kv_local // 2, 16, width), bf16),
            pltpu.VMEM((kv_local // 2, 2, n_x, n_j, 16, width), bf16),
            pltpu.VMEM((2, 8, rows, width), bf16),
            pltpu.VMEM((keys // chunk, rows, chunk), f32),
            per_row,
            per_row,
            per_row,
            pltpu.VMEM((3, rows, width), f32),
            per_row,
            pltpu.VMEM((8, 128), f32),
            pltpu.VMEM((n_i, 8, 128), f32),
            pltpu.VMEM((kv_local, SAMPLES, 16, width), bf16),
            pltpu.VMEM((kv_local, n_i, 16, width), bf16),
            pltpu.VMEM((SAMPLES, 8, 128), f32),
            pltpu.VMEM((n_i, 8, 128), f32),
            pltpu.VMEM((SAMPLES, 2, 128), f32),
            pltpu.VMEM((n_i, 2, 128), f32),
            pltpu.VMEM((n_x, kv_local * 8, width), f32),
            pltpu.VMEM((n_x, kv_local * 8, width), f32),
            pltpu.VMEM((n_x, 16, width), f32),
            pltpu.VMEM((n_x, 16, width), f32),
            dma((len(ints),)),
            dma((2,)),
            dma((kv_local,)),
            dma,
            dma((kv_local // 2, n_x)),
            dma((kv_local // 2, n_x)),
            dma((kv_local // 2, n_x)),
            dma((kv_local // 2, n_x)),
            dma,
            dma,
            dma((kv_local,)),
            dma((kv_local,)),
            dma,
            dma,
            dma,
            dma,
            dma,
            dma,
            dma,
            dma,
        ],
        compiler_params=pltpu.CompilerParams(
            collective_id=0, has_side_effects=True, vmem_limit_bytes=60 << 20
        ),
        name="decode_attention",
    )(*ints, q, new, suffix, prefix_kv)
    return out.reshape(steps, rows_dev, heads * width)


def solution(mesh):
    return jax.shard_map(
        functools.partial(local, mesh.shape["rows"], mesh.shape["prefix"]),
        mesh=mesh,
        in_specs=(
            P(None, ("rows", "prefix"), None, None),
            P(None, None, ("rows", "prefix"), None, None),
            P(None, ("rows", "prefix"), None, None, None),
            P(("rows", "prefix")),
            P(),
            P(None, "prefix", "rows", None, None),
            P("prefix", None),
            P("prefix", None),
            P("prefix"),
        ),
        out_specs=P(None, ("rows", "prefix"), None),
        check_vma=False,
    )
```

```python
import functools
import math

import jax
import jax.numpy as jnp
from jax import lax
from jax.experimental import pallas as pl
from jax.experimental.pallas import tpu as pltpu
from jax.sharding import PartitionSpec as P

MESH = pl.DeviceIdType.MESH
SAMPLES = 16
masked_score = -1e30
exponent = 168.0 ** (-0.5) * math.log2(math.e)
f32 = jnp.float32
bf16 = jnp.bfloat16
NT = (((1,), (1,)), ((), ()))
NN = (((1,), (0,)), ((), ()))
X_ORDER = (0, 1, 3, 2)


def far_first(n_i):
    n = n_i // 8

    def hops(d):
        z, y = d // 8, d % 8 // 2
        return min(z, n - z) + min(y, 4 - y)

    return sorted(range(1, n_i), key=hops, reverse=True)


def iota(shape, dim):
    return lax.broadcasted_iota(jnp.int32, shape, dim)


def kernel(
    n_x,
    n_i,
    block_len,
    slots,
    prompt_hbm,
    index_hbm,
    count_hbm,
    prefix_len_hbm,
    suffix_len_hbm,
    q_hbm,
    new_hbm,
    suffix_hbm,
    prefix_hbm,
    out_ref,
    prompt_ref,
    index_ref,
    count_ref,
    prefix_len_ref,
    suffix_len_ref,
    q_ref,
    new_ref,
    kv,
    suf,
    q_own,
    q_all,
    q_prompt,
    own_s,
    own_acc,
    own_m,
    own_l,
    m_sel,
    packed,
    tag,
    tag_in,
    part,
    part_in,
    stat,
    stat_in,
    last_stat,
    last_stat_in,
    fin,
    fin_in,
    last_fin,
    last_fin_in,
    int_sem,
    small_sem,
    kv_sem,
    suf_sem,
    q_send,
    q_recv,
    forward_send,
    forward_recv,
    tag_send,
    tag_recv,
    part_send,
    part_recv,
    stat_send,
    stat_recv,
    last_stat_send,
    last_stat_recv,
    fin_send,
    fin_recv,
    last_fin_send,
    last_fin_recv,
):
    me_x = lax.axis_index("rows")
    me_i = lax.axis_index("prefix")
    me_j = me_i // 2
    me_c = lax.rem(me_i, 2)
    other_c = 1 - me_c
    sibling = (me_x, me_j * 2 + other_c)
    n_j = n_i // 2
    kv_local = kv.shape[0]
    rows = q_ref.shape[0]
    half_j = SAMPLES // 2
    lane = iota((1, 128), 1)
    pairs = kv_local // 2

    def peer(d):
        to = me_i + d
        return jnp.where(to >= n_i, to - n_i, to)

    me_sample = lax.rem(me_i, SAMPLES)

    def sample(d):
        n = me_sample + d % SAMPLES
        return jnp.where(n >= SAMPLES, n - SAMPLES, n)

    def on_core(d):
        to = me_i + 2 * d
        return jnp.where(to >= n_i, to - n_i, to)

    def mate(d):
        to = me_x + d
        return jnp.where(to >= n_x, to - n_x, to)

    barrier = pltpu.get_barrier_semaphore()
    for j in range(n_j):
        pl.semaphore_signal(
            barrier, inc=1, device_id=(me_x, j * 2 + other_c), device_id_type=MESH
        )
    for dx in range(n_x):

        for d in range(1 if dx == 0 else 0, n_j):
            pl.semaphore_signal(
                barrier, inc=1, device_id=(mate(dx), on_core(d)), device_id_type=MESH
            )

    small_copies = [
        pltpu.make_async_copy(q_hbm, q_ref, small_sem.at[0]),
        pltpu.make_async_copy(new_hbm, new_ref, small_sem.at[1]),
    ]
    int_copies = [
        pltpu.make_async_copy(src, dst, int_sem.at[n])
        for n, (src, dst) in enumerate(
            (
                (prompt_hbm, prompt_ref),
                (index_hbm, index_ref),
                (count_hbm, count_ref),
                (prefix_len_hbm, prefix_len_ref),
                (suffix_len_hbm, suffix_len_ref),
            )
        )
    ]
    suf_copy = pltpu.make_async_copy(suffix_hbm, suf, suf_sem)
    kv_copies = [
        pltpu.make_async_copy(prefix_hbm.at[:, :, k], kv.at[k], kv_sem.at[k])
        for k in range(kv_local)
    ]
    for copy in small_copies + int_copies + [suf_copy]:
        copy.start()

    r = iota((rows, rows), 0)
    c = iota((rows, rows), 1)
    source = lax.rem(r, 4) * 32 + (r // 8) * 2 + lax.rem(r // 4, 2)
    order = jnp.where(c == source, 1.0, 0.0).astype(bf16)
    small_copies[0].wait()
    q_mine = lax.dot_general(order, q_ref[...], NN, preferred_element_type=f32).astype(bf16)
    q_own[...] = q_mine.reshape(n_x, pairs, 16, 128)
    for pair in range(pairs):
        q_all[pair, me_c, me_x, me_j] = q_own[me_x, pair]
    packed[...] = jnp.zeros_like(packed)

    pl.semaphore_wait(barrier, n_x * n_j - 1 + n_j)

    def waiter(ref, send, recv):
        return pltpu.make_async_remote_copy(
            src_ref=ref,
            dst_ref=ref,
            send_sem=send,
            recv_sem=recv,
            device_id=sibling,
            device_id_type=MESH,
        )

    def push(src, dst, send, recv, to):
        pltpu.make_async_remote_copy(
            src_ref=src,
            dst_ref=dst,
            send_sem=send,
            recv_sem=recv,
            device_id=to,
            device_id_type=MESH,
        ).start()

    def push_pair(pair):
        for dx in X_ORDER:
            x = mate(dx)
            for d in range(1 if dx == 0 else 0, n_j):
                push(
                    q_own.at[x, pair],
                    q_all.at[pair, me_c, me_x, me_j],
                    q_send.at[pair, dx],
                    q_recv.at[pair, dx],
                    (x, on_core(d)),
                )

    push_pair(0)
    for copy in kv_copies:
        copy.start()

    def q_wait(pair, dx):
        chunks = q_all.at[pair, me_c, 0, pl.ds(0, n_j - 1 if dx == 0 else n_j)]
        return waiter(chunks, q_send.at[pair, dx], q_recv.at[pair, dx])

    for copy in small_copies[1:] + int_copies + [suf_copy]:
        copy.wait()
    count = count_ref[0]
    prompt_a = prompt_ref[0, 0]
    prompt_b = prompt_ref[0, jnp.maximum(count - 1, 0)]
    base = lax.rem(me_i, 8) * 16
    in_first = (lane >= base) & (lane < base + 8)
    in_second = (lane >= base + 8) & (lane < base + 16)
    tag_a = prompt_a.astype(f32)
    tag_b = jnp.where(prompt_b == prompt_a, -1, prompt_b).astype(f32)
    tags = jnp.where(in_first, tag_a, jnp.where(in_second, tag_b, 0.0))
    tag[...] = jnp.broadcast_to(tags, (8, 128))
    tag_in[me_i] = tag[...]

    chunk = own_s.shape[2]
    chunks = own_s.shape[0]
    suffix_len = suffix_len_ref[0]
    row_head = iota((rows, 1), 0) // 8
    row_step = lax.rem(iota((rows, 1), 0), 4)
    near = lax.dot_general(q_mine, new_ref[0], NT, preferred_element_type=f32)
    key = iota((1, near.shape[1]), 1)
    near_live = (lax.rem(key, 16) == row_head) & (key // 16 <= row_step)
    near = jnp.where(near_live, near, masked_score)
    key = iota((1, chunk), 1)
    same_head = lax.rem(key, 16) == row_head

    def far_scores(n, peak):
        s = lax.dot_general(
            q_mine, suf[0, pl.ds(n * chunk, chunk)], NT, preferred_element_type=f32
        )
        live = same_head & (n * (chunk // 16) + key // 16 < suffix_len)
        s = jnp.where(live, s, masked_score)
        own_s[n] = s
        return jnp.maximum(peak, jnp.max(s, axis=1, keepdims=True))

    own_peak = lax.fori_loop(0, chunks, far_scores, jnp.max(near, axis=1, keepdims=True))
    near_w = jnp.exp2((near - own_peak) * exponent).astype(bf16)
    near_sum = lax.dot_general(near_w, new_ref[1], NN, preferred_element_type=f32)
    near_mass = jnp.sum(near_w.astype(f32), axis=1, keepdims=True)
    ones = jnp.ones((chunk, 128), bf16)

    def far_sums(n, carry):
        total, mass = carry
        w = jnp.exp2((own_s[n] - own_peak) * exponent).astype(bf16)
        values = jnp.concatenate([suf[1, pl.ds(n * chunk, chunk)], ones], axis=1)
        both = lax.dot_general(w, values, NN, preferred_element_type=f32)
        return total + both[:, :128], mass + both[:, 128:]

    total, mass = lax.fori_loop(
        0, chunks, far_sums, (near_sum, jnp.broadcast_to(near_mass, (rows, 128)))
    )
    own_acc[...] = total
    own_l[...] = mass
    own_m[...] = jnp.broadcast_to(own_peak, (rows, 128))

    push_pair(1)

    column = iota((1, block_len), 1)
    ones = jnp.ones((block_len, 128), bf16)
    in_a = [jnp.where(prompt_ref[0, j] == prompt_a, 1, 0) for j in range(slots)]
    outside_a = outside_b = jnp.full((1, 128), masked_score, f32)
    for j in range(slots):
        inside = jnp.where(prompt_ref[0, j] == prompt_a, 0.0, masked_score)
        outside_a = jnp.where(lane == j, inside, outside_a)
        inside = jnp.where(prompt_ref[0, j] == prompt_b, 0.0, masked_score)
        outside_b = jnp.where(lane == j, inside, outside_b)

    def forward_q(pair):
        for dx in X_ORDER:
            q_wait(pair, dx).wait_recv()
            mine = q_all.at[pair, me_c, lax.rem(me_x + n_x - dx, n_x)]
            push(mine, mine, forward_send.at[pair, dx], forward_recv.at[pair, dx], sibling)

    def push_part(k):
        for d in far_first(n_i):
            push(
                part.at[k, sample(d)],
                part_in.at[k, me_i],
                part_send.at[k],
                part_recv.at[k],
                (me_x, peer(d)),
            )
        part_in[k, me_i] = part[k, me_sample]

    def push_stats(last):
        here, there = (last_stat, last_stat_in) if last else (stat, stat_in)
        send, recv = (last_stat_send, last_stat_recv) if last else (stat_send, stat_recv)
        turned = packed[...].T
        first = pltpu.roll(turned[:8], base, 1)
        second = pltpu.roll(turned[8:16], base + 8, 1)
        for n in range(SAMPLES):
            shift = (128 - 8 * n) % 128
            one, two = (pltpu.roll(a, shift, 1) if shift else a for a in (first, second))
            both = jnp.where(in_first, one, jnp.where(in_second, two, 0.0))
            here[n] = both[6:8] if last else both

        for d in far_first(n_i):
            push(here.at[sample(d)], there.at[me_i], send, recv, (me_x, peer(d)))
        there[me_i] = here[me_sample]

    forward_q(0)
    for d in range(1, n_i):
        push(tag, tag_in.at[me_i], tag_send, tag_recv, (me_x, peer(d)))
    for copy in kv_copies:
        copy.wait()
    for k in range(kv_local):
        pair = k // 2
        if k % 2 == 0:
            for dx in X_ORDER:
                waiter(
                    q_all.at[pair, me_c, 0], forward_send.at[pair, dx], forward_recv.at[pair, dx]
                ).wait_recv()
            for half in range(2):
                for x in range(n_x):
                    v = q_all[pair, :, x, pl.ds(half * half_j, half_j)].astype(f32)
                    v = v.swapaxes(0, 1).reshape(SAMPLES, 2, 8, 128)
                    for n in range(2):
                        q_prompt[n, 2 * x + half] = v[:, n].reshape(rows, 128).astype(bf16)

        accs, ms = [], []
        peaks = jnp.full((rows, 128), masked_score, f32)
        masses = jnp.zeros((rows, 128), f32)
        for j in range(slots):
            prompt = prompt_ref[0, j]
            live = prefix_len_ref[prompt] - index_ref[0, j] * block_len
            live = jnp.where(j < count, live, 0)
            s = lax.dot_general(
                q_prompt[k % 2, prompt], kv[k, 0, j], NT, preferred_element_type=f32
            )
            s = jnp.where(column < live, s, masked_score)
            m = jnp.max(s, axis=1, keepdims=True)
            w = jnp.exp2((s - m) * exponent).astype(bf16)
            values = jnp.concatenate([kv[k, 1, j], ones], axis=1)
            both = lax.dot_general(w, values, NN, preferred_element_type=f32)
            accs.append(both[:, :128])
            ms.append(m)
            peaks = jnp.where(lane == j, m, peaks)
            masses = jnp.where(lane == j, both[:, 128:], masses)

        pack = packed[...]
        for place, outside in ((1, outside_a), (2, outside_b)):
            shifted = peaks + outside
            peak = jnp.max(shifted, axis=1, keepdims=True)
            take = jnp.exp2((shifted - peak) * exponent)
            mass = jnp.sum(take * masses, axis=1, keepdims=True)
            m_sel[place] = jnp.broadcast_to(peak, (rows, 128))
            at = (place - 1) * 8 + k * 2
            pack = jnp.where(lane == at, peak, jnp.where(lane == at + 1, mass, pack))
        packed[...] = pack
        total_a = total_b = jnp.zeros((rows, 128), f32)
        for j in range(slots):
            take = jnp.exp2((ms[j] - m_sel[2 - in_a[j]]) * exponent)
            taken = take * accs[j]
            total_a = total_a + jnp.where(in_a[j] == 1, taken, 0.0)
            total_b = total_b + jnp.where(in_a[j] == 1, 0.0, taken)
        parts = [t.reshape(SAMPLES, 8, 128) for t in (total_a, total_b)]
        part[k] = jnp.concatenate(parts, axis=1).astype(bf16)
        if k == 0:
            forward_q(1)
        push_part(k)
        if k >= kv_local - 2:
            push_stats(k == kv_local - 1)

    tag_wait = waiter(tag_in.at[pl.ds(0, n_i - 1)], tag_send, tag_recv)
    tag_wait.wait_recv()
    part_waits = [
        waiter(part_in.at[k, pl.ds(0, n_i - 1)], part_send.at[k], part_recv.at[k])
        for k in range(kv_local)
    ]
    stat_wait = waiter(stat_in.at[pl.ds(0, n_i - 1)], stat_send, stat_recv)
    last_stat_wait = waiter(
        last_stat_in.at[pl.ds(0, n_i - 1)], last_stat_send, last_stat_recv
    )

    def side_by_side(ref):
        groups = [functools.reduce(jnp.add, [ref[g * 8 + n] for n in range(8)]) for g in range(n_i // 8)]
        return jnp.concatenate(groups, axis=1)

    key = iota((1, n_i * 16), 1)
    row = iota((n_x * 8, 1), 0)
    prompt = (row // 8 * 2 + lax.rem(me_i // SAMPLES, 2)).astype(f32)
    same = (lax.rem(key, 8) == lax.rem(row, 8)) & (side_by_side(tag_in)[:1] == prompt)

    def combine(k, st):
        part_waits[k].wait_recv()
        peaks = jnp.where(same, st[:1], masked_score)
        peak = jnp.max(peaks, axis=1, keepdims=True)
        factor = jnp.where(same, jnp.exp2((peaks - peak) * exponent), 0.0)
        mass = jnp.sum(factor * st[1:], axis=1, keepdims=True)
        high = factor.astype(bf16)
        low = (factor - high.astype(f32)).astype(bf16)
        parts = part_in[k].reshape(n_i * 16, 128)
        total = lax.dot_general(high, parts, NN, preferred_element_type=f32)
        total = total + lax.dot_general(low, parts, NN, preferred_element_type=f32)
        return total.reshape(n_x, 8, 128), peak, mass

    def push_fin(here, there, send, recv):
        for d in range(1, n_x):
            x = mate(d)
            push(here.at[x], there.at[me_x], send, recv, (x, me_i))
        there[me_x] = here[me_x]
        return waiter(there.at[pl.ds(0, n_x - 1)], send, recv)

    def finish(g, k, total, st, at):
        span = pl.ds((g * kv_local + k) * 8, 8)
        prefix_peak = st[:, at : at + 1]
        prefix_mass = st[:, at + 1 : at + 2]
        peak = own_m[span, :]
        top = jnp.maximum(prefix_peak, peak)
        from_prefix = jnp.exp2((prefix_peak - top) * exponent)
        from_own = jnp.exp2((peak - top) * exponent)
        numer = from_prefix * total + from_own * own_acc[span, :]
        denom = from_prefix * prefix_mass + from_own * own_l[span, :]
        result = (numer / denom).astype(bf16)
        for n in range(2):
            head = (g * kv_local + k) * 2 + n
            out_ref[:, head * 128 : head * 128 + 128] = result[n * 4 : n * 4 + 4]

    early = kv_local - 1
    stat_wait.wait_recv()
    st = side_by_side(stat_in)
    tile = jnp.zeros((n_x * 8, 128), f32)
    for k in range(early):
        total, peak, mass = combine(k, st[k * 2 : k * 2 + 2])
        fin[:, k * 8 : k * 8 + 8] = total
        tile = jnp.where(lane == k * 2, peak, jnp.where(lane == k * 2 + 1, mass, tile))
    fin[:, early * 8 : early * 8 + 8] = tile.reshape(n_x, 8, 128)
    fin_wait = push_fin(fin, fin_in, fin_send, fin_recv)

    last_stat_wait.wait_recv()
    total, peak, mass = combine(early, side_by_side(last_stat_in))
    last_fin[:, :8] = total
    tile = jnp.where(lane == 0, peak, jnp.where(lane == 1, mass, 0.0))
    last_fin[:, 8:16] = tile.reshape(n_x, 8, 128)
    last_fin_wait = push_fin(last_fin, last_fin_in, last_fin_send, last_fin_recv)

    fin_wait.wait_recv()
    for g in range(n_x):
        st = fin_in[g, early * 8 : early * 8 + 8]
        for k in range(early):
            finish(g, k, fin_in[g, k * 8 : k * 8 + 8], st, k * 2)
    last_fin_wait.wait_recv()
    for g in range(n_x):
        finish(g, early, last_fin_in[g, :8], last_fin_in[g, 8:16], 0)

    for pair in range(pairs):
        for dx in range(n_x):
            q_wait(pair, dx).wait_send()
            waiter(
                q_all.at[pair, me_c, 0], forward_send.at[pair, dx], forward_recv.at[pair, dx]
            ).wait_send()
    for k in range(kv_local):
        part_waits[k].wait_send()
    tag_wait.wait_send()
    stat_wait.wait_send()
    last_stat_wait.wait_send()
    fin_wait.wait_send()
    last_fin_wait.wait_send()


def local(
    n_x,
    n_i,
    queries,
    new_kv,
    suffix_kv,
    suffix_len,
    prefix_len,
    prefix_kv,
    block_prompt,
    block_index,
    block_count,
):
    steps, rows_dev, heads, width = queries.shape
    slots, kv_local, block_len = prefix_kv.shape[1:4]
    rows = steps * heads
    n_j = n_i // 2
    q = queries.reshape(rows, width)
    new = new_kv.reshape(2, -1, width)
    suffix = suffix_kv.reshape(2, -1, width)
    keys = suffix.shape[1]
    chunk = 1024
    ints = (block_prompt, block_index, block_count, prefix_len, suffix_len)
    hbm = pl.BlockSpec(memory_space=pl.ANY)
    dma = pltpu.SemaphoreType.DMA
    per_row = pltpu.VMEM((rows, width), f32)
    out = pl.pallas_call(
        functools.partial(kernel, n_x, n_i, block_len, slots),
        out_shape=jax.ShapeDtypeStruct((steps, heads * width), bf16),
        in_specs=[hbm] * 9,
        out_specs=pl.BlockSpec(memory_space=pltpu.VMEM),
        scratch_shapes=[pltpu.SMEM(a.shape, a.dtype) for a in ints]
        + [
            pltpu.VMEM(q.shape, bf16),
            pltpu.VMEM(new.shape, bf16),
            pltpu.VMEM((kv_local, 2, slots, block_len, width), bf16),
            pltpu.VMEM((2, keys, width), bf16),
            pltpu.VMEM((n_x, kv_local // 2, 16, width), bf16),
            pltpu.VMEM((kv_local // 2, 2, n_x, n_j, 16, width), bf16),
            pltpu.VMEM((2, 8, rows, width), bf16),
            pltpu.VMEM((keys // chunk, rows, chunk), f32),
            per_row,
            per_row,
            per_row,
            pltpu.VMEM((3, rows, width), f32),
            per_row,
            pltpu.VMEM((8, 128), f32),
            pltpu.VMEM((n_i, 8, 128), f32),
            pltpu.VMEM((kv_local, SAMPLES, 16, width), bf16),
            pltpu.VMEM((kv_local, n_i, 16, width), bf16),
            pltpu.VMEM((SAMPLES, 8, 128), f32),
            pltpu.VMEM((n_i, 8, 128), f32),
            pltpu.VMEM((SAMPLES, 2, 128), f32),
            pltpu.VMEM((n_i, 2, 128), f32),
            pltpu.VMEM((n_x, kv_local * 8, width), f32),
            pltpu.VMEM((n_x, kv_local * 8, width), f32),
            pltpu.VMEM((n_x, 16, width), f32),
            pltpu.VMEM((n_x, 16, width), f32),
            dma((len(ints),)),
            dma((2,)),
            dma((kv_local,)),
            dma,
            dma((kv_local // 2, n_x)),
            dma((kv_local // 2, n_x)),
            dma((kv_local // 2, n_x)),
            dma((kv_local // 2, n_x)),
            dma,
            dma,
            dma((kv_local,)),
            dma((kv_local,)),
            dma,
            dma,
            dma,
            dma,
            dma,
            dma,
            dma,
            dma,
        ],
        compiler_params=pltpu.CompilerParams(
            collective_id=0, has_side_effects=True, vmem_limit_bytes=60 << 20
        ),
        name="decode_attention",
    )(*ints, q, new, suffix, prefix_kv)
    return out.reshape(steps, rows_dev, heads * width)


def solution(mesh):
    return jax.shard_map(
        functools.partial(local, mesh.shape["rows"], mesh.shape["prefix"]),
        mesh=mesh,
        in_specs=(
            P(None, ("rows", "prefix"), None, None),
            P(None, None, ("rows", "prefix"), None, None),
            P(None, ("rows", "prefix"), None, None, None),
            P(("rows", "prefix")),
            P(),
            P(None, "prefix", "rows", None, None),
            P("prefix", None),
            P("prefix", None),
            P("prefix"),
        ),
        out_specs=P(None, ("rows", "prefix"), None),
        check_vma=False,
    )
```
